32 devices in a mesh: gx: 8 (over z, x), gy: 4 (over y, core).
Axes of the slice: x: 2, y: 2, z: 4, core: 2. Of those that a mesh axis runs over, the one named last changes fastest.
Arguments:
- prediction: float32 [128, 64, 128], P('gx', 'gy'), may hold values from 0 to 1
- label_mask: int32 [128, 64, 128], P('gx', 'gy'), may hold values 0 or 1
- confidence: float32 [128, 64, 128], P('gx', 'gy'), may hold values from 0.5 to 1
Outputs:
- gradient: float32 [128, 64, 128], P('gx', 'gy')
- loss: float32 [], replicated
The draws below stay inside these ranges and needn't reach their ends.
All inputs are finite; a program needn't handle non-finite values. No bound on the sum of `label_mask` on one device may be relied on, other than what follows from the above.
Results may differ from the reference program's by a relative error of at most 0.000025.
Values sent between devices are 32-bit elements; how exact they have to be, the bound alone decides.
A program may use at most 128 MiB of HBM per device.

```python
from functools import partial
import jax
import jax.numpy as jnp
from jax import lax

NZ = 128
ITERS = 3
NX = 128
NY = 64


def place_ends(drawn, stream_key, smallest, top_value):
    dims = drawn.shape
    place = [jax.random.randint(jax.random.fold_in(stream_key, axis), (), 0, dims[axis]) for axis in range(len(dims))]
    drawn = drawn.at[tuple(place)].set(smallest)
    longest = dims.index(max(dims))
    place[longest] = (place[longest] + 1) % dims[longest]
    return drawn.at[tuple(place)].set(top_value)


def block_scale(stream_key, dims, shards, low, high):
    factor_of, own = 1.0, jax.random.fold_in(stream_key, 6)
    for position, parts in shards:
        draws = jnp.exp(jax.random.uniform(jax.random.fold_in(own, position), (parts,), jnp.float32, low / len(shards), high / len(shards)))
        factor_of = factor_of * jnp.repeat(draws, dims[position] // parts).reshape([-1 if axis == position else 1 for axis in range(len(dims))])
    return factor_of


def setup_inputs(seed: int = 0) -> dict:
    seeds = jax.random.split(jax.random.key(seed), 4)
    prediction = jnp.clip(1.0 * jax.random.uniform(seeds[0], (NX, NY, NZ), jnp.float32) ** block_scale(seeds[0], (NX, NY, NZ), ((0, 8), (1, 4)), -0.2, 0.2), 0.0, 1.0)
    label_mask = place_ends((jax.random.randint(seeds[1], (NX, NY, NZ), 0, 2) < 1).astype(jnp.int32), jax.random.fold_in(seeds[1], 1), 0, 1)
    confidence = jnp.clip(0.5 + 0.5 * jax.random.uniform(seeds[2], (NX, NY, NZ), jnp.float32) ** block_scale(seeds[2], (NX, NY, NZ), ((0, 8), (1, 4)), -0.2, 0.2), 0.5, 1.0)
    return {"prediction": prediction, "label_mask": label_mask, "confidence": confidence}


def sides(volume, axis, first, last):
    widths = [(0, 0), (0, 0), (0, 0)]
    widths[axis] = (1, 1)
    padded = jnp.pad(volume, widths, mode='edge')
    length = volume.shape[axis]
    lower = lax.slice_in_dim(padded, 0, length, axis=axis)
    upper = lax.slice_in_dim(padded, 2, length + 2, axis=axis)
    if first is not None:
        lower = jnp.where(first, volume, lower)
        upper = jnp.where(last, volume, upper)
    return (lower, upper)

def pooled(volume, axis, first, last, picker):
    lower, upper = sides(volume, axis, first, last)
    return picker(picker(lower, volume), upper)

def erode(volume, edges):
    along_one = pooled(volume, 0, edges[0], edges[1], jnp.minimum)
    along_two = pooled(volume, 1, edges[2], edges[3], jnp.minimum)
    along_three = pooled(volume, 2, None, None, jnp.minimum)
    return jnp.minimum(jnp.minimum(along_one, along_two), along_three)

def dilate(volume, edges):
    result = pooled(volume, 0, edges[0], edges[1], jnp.maximum)
    result = pooled(result, 1, edges[2], edges[3], jnp.maximum)
    return pooled(result, 2, None, None, jnp.maximum)

def skel_step(state, edges):
    volume, skeleton_sum = state
    eroded = erode(volume, edges)
    delta = jax.nn.relu(volume - dilate(eroded, edges))
    skeleton_sum = skeleton_sum + jax.nn.relu(delta - skeleton_sum * delta)
    return (eroded, skeleton_sum)

def skeleton(volume, edges):
    eroded = erode(volume, edges)
    skeleton_sum = jax.nn.relu(volume - dilate(eroded, edges))
    state = (eroded, skeleton_sum)
    stepper = jax.checkpoint(partial(skel_step, edges=edges))
    for index in range(ITERS):
        state = stepper(state)
    return state[1]

def reference(prediction, label_mask, confidence):
    edges = (None, None, None, None)
    target = label_mask.astype(jnp.float32) * confidence
    skel_pred, pullback = jax.vjp(lambda volume: skeleton(volume, edges), prediction)
    skel_target = skeleton(target, edges)
    sum_a = jnp.sum(skel_pred * target)
    sum_b = jnp.sum(skel_pred)
    sum_c = jnp.sum(skel_target * prediction)
    sum_d = jnp.sum(skel_target)
    precision = (sum_a + 1.0) / (sum_b + 1.0)
    sensitivity = (sum_c + 1.0) / (sum_d + 1.0)
    together = precision + sensitivity
    loss = 1.0 - 2.0 * precision * sensitivity / together
    cells = jnp.float32(NX * NY * NZ)
    coef_pred = cells * (-2.0 * sensitivity * sensitivity / (together * together)) / (sum_b + 1.0)
    coef_target = cells * (-2.0 * precision * precision / (together * together)) / (sum_d + 1.0)
    cotangent = coef_pred * (target - precision)
    gradient = pullback(cotangent)[0] + coef_target * skel_target
    return (gradient, loss)
```

```python
import functools

import jax
import jax.numpy as jnp
from jax import lax
from jax.experimental import pallas as pl
from jax.experimental.pallas import tpu as pltpu
from jax.sharding import PartitionSpec as P

ITERS = 3
STAGES = ITERS + 1
DEPTH = ITERS + 2
XO = 8
YE = 8
YW = 12
MESH = pl.DeviceIdType.MESH
XL, XU, YL, YU, ZL, ZU, CC = range(7)
LO, UP, MID = range(3)
DIRS = ((-1, 0), (1, 0), (0, -1), (0, 1), (-1, -1), (-1, 1), (1, -1), (1, 1))


def share(winner, other):
    return jnp.where(winner < other, 1.0, jnp.where(winner == other, 0.5, 0.0))


def loop(low, high, body, step=2):
    count = (high - low) // step

    @pl.loop(0, count)
    def _(index):
        for k in range(step):
            body(low + index * step + k)

    for row in range(low + count * step, high):
        body(row)


def kernel(
    sizes, pred_hbm, label_hbm, conf_hbm, out, loss,
    vol, lab, conf, skel, dels, befores, coefs, pool, wgt, wx, wy, wz, grad, hz, hy, final,
    part, slots_y, slots_x, got_x, got_y, got_c,
    in_sem, halo_send, halo_recv, sy_send, sy_recv, sx_send, sx_recv, g_send, g_recv,
):
    rows, cols, planes, ngx, ngy = sizes
    gx, gy = lax.axis_index("gx"), lax.axis_index("gy")
    own_x, own_y, own_w = pl.ds(XO, rows), pl.ds(YE, cols), pl.ds(YW, cols)
    span = cols + 8
    lanes = lax.broadcasted_iota(jnp.int32, (1, planes), 1)
    at_first, at_last = lanes == 0, lanes == planes - 1

    loads = [
        pltpu.make_async_copy(pred_hbm, vol.at[0, 0, own_x, own_y], in_sem.at[0]),
        pltpu.make_async_copy(label_hbm, lab, in_sem.at[1]),
        pltpu.make_async_copy(conf_hbm, conf, in_sem.at[2]),
    ]
    for copy in loads:
        copy.start()

    def there(dx, dy):
        found = None
        for d, me, size in ((dx, gx, ngx), (dy, gy, ngy)):
            if d:
                inside = (me > 0) if d < 0 else (me < size - 1)
                found = inside if found is None else jnp.logical_and(found, inside)
        return found

    barrier = pltpu.get_barrier_semaphore()
    for k in range(1, ngx):
        pl.semaphore_signal(barrier, inc=1, device_id=(lax.rem(gx + k, ngx), gy), device_id_type=MESH)
    for k in range(1, ngy):
        pl.semaphore_signal(barrier, inc=1, device_id=(gx, lax.rem(gy + k, ngy)), device_id_type=MESH)
    for dx, dy in DIRS[4:]:
        @pl.when(there(dx, dy))
        def _(dx=dx, dy=dy):
            pl.semaphore_signal(barrier, inc=1, device_id=(gx + dx, gy + dy), device_id_type=MESH)

    for copy in loads:
        copy.wait()

    def make_target(row):
        vol[0, 1, XO + row, YE : YE + cols] = lab[row].astype(jnp.float32) * conf[row]

    loop(0, rows, make_target)

    corners = 1
    for me, size in ((gx, ngx), (gy, ngy)):
        corners *= lax.div(me + size - 1, size) + lax.div(2 * size - 2 - me, size)
    pl.semaphore_wait(barrier, ngx - 1 + ngy - 1 + corners)

    def strip(d, length, offset, width, outside):
        if d == 0:
            return pl.ds(offset, length)
        if d < 0:
            return pl.ds(offset - width if outside else offset, width)
        return pl.ds(offset + length if outside else offset + length - width, width)

    halos = []
    for k, (dx, dy) in enumerate(DIRS):
        copy = pltpu.make_async_remote_copy(
            src_ref=vol.at[0, :, strip(dx, rows, XO, DEPTH, False), strip(dy, cols, YE, 8, False)],
            dst_ref=vol.at[0, :, strip(-dx, rows, XO, DEPTH, True), strip(-dy, cols, YE, 8, True)],
            send_sem=halo_send.at[k],
            recv_sem=halo_recv.at[k],
            device_id=(gx + dx, gy + dy),
            device_id_type=MESH,
        )
        halos.append(copy)
        pl.when(there(dx, dy))(copy.start)

    def clear_grad(row):
        for i in range(STAGES + 1):
            grad[i, row] = jnp.zeros((cols + 24, planes), jnp.float32)

    loop(XO - DEPTH - 1, XO + rows + DEPTH + 1, clear_grad)
    for i in range(STAGES):
        reach = STAGES - i
        for row in (XO - reach - 2, XO - reach - 1, XO + rows + reach, XO + rows + reach + 1):
            for kind in range(7):
                wgt[i, kind, row] = jnp.zeros((cols + 24, planes), jnp.float32)
        for row in (XO - 2, XO - 1, XO + rows, XO + rows + 1):
            hy[i, row] = jnp.zeros((span, planes), jnp.float32)
            for kind in range(3):
                wx[i, kind, row] = jnp.zeros((span, planes), jnp.float32)

    tile = jnp.zeros((8, planes), jnp.float32)

    def clear_sides(row):
        for i in range(STAGES):
            for kind in range(7):
                if i == 0 or kind == YU:
                    wgt[i, kind, row, 0:8] = tile
                if i == 0 or kind == YL:
                    wgt[i, kind, row, cols + 16 : cols + 24] = tile

    loop(XO - STAGES, XO + rows + STAGES, clear_sides)

    def clear_pools(row):
        for i in range(STAGES):
            hz[i, row, YW - 8 : YW] = tile
            hz[i, row, YW + cols : YW + cols + 8] = tile
            for kind in range(3):
                wy[i, kind, row, YW - 8 : YW] = tile
                wy[i, kind, row, YW + cols : YW + cols + 8] = tile

    loop(0, rows, clear_pools)

    for k, (dx, dy) in enumerate(DIRS):
        pl.when(there(-dx, -dy))(halos[k].wait_recv)

    def stand_in(i):
        reach = DEPTH - i
        every = pl.ds(XO - reach, rows + 2 * reach)

        @pl.when(gy == 0)
        def _():
            vol[i, :, every, YE - 1 : YE] = vol[i, :, every, YE : YE + 1]

        @pl.when(gy == ngy - 1)
        def _():
            vol[i, :, every, YE + cols : YE + cols + 1] = vol[i, :, every, YE + cols - 1 : YE + cols]

        @pl.when(gx == 0)
        def _():
            vol[i, :, XO - 1] = vol[i, :, XO]

        @pl.when(gx == ngx - 1)
        def _():
            vol[i, :, XO + rows] = vol[i, :, XO + rows - 1]

    def before(value, edge):
        return jnp.where(at_first, edge, pltpu.roll(value, 1, 1))

    def after(value):
        return jnp.where(at_last, value, pltpu.roll(value, planes - 1, 1))

    def erode_step(i):
        reach = STAGES - i

        def step(row):
            for v in range(2):
                mid = vol[i, v, row, 4 : 4 + span]
                least = jnp.minimum(vol[i, v, row - 1, 4 : 4 + span], vol[i, v, row + 1, 4 : 4 + span])
                sides = jnp.minimum(vol[i, v, row, 3 : 3 + span], vol[i, v, row, 5 : 5 + span])
                along = jnp.minimum(before(mid, mid), after(mid))
                vol[i + 1, v, row, 4 : 4 + span] = jnp.minimum(jnp.minimum(least, sides), jnp.minimum(along, mid))

        loop(XO - reach, XO + rows + reach, step)
        stand_in(i + 1)

    def delta_step(i):
        def step(row):
            for v in range(2):
                most = None
                for x in (-1, 0, 1):
                    for y in (-1, 0, 1):
                        value = vol[i + 1, v, XO + row + x, YE + y : YE + y + cols]
                        most = value if most is None else jnp.maximum(most, value)
                most = jnp.maximum(jnp.maximum(before(most, most), most), after(most))
                delta = jnp.maximum(vol[i, v, XO + row, YE : YE + cols] - most, 0.0)
                if i == 0:
                    result = delta
                else:
                    old = skel[v, row]
                    result = old + jnp.maximum(delta - old * delta, 0.0)
                skel[v, row] = result
                if v == 0:
                    dels[i, row] = delta
                    if i > 0:
                        befores[i, row] = old

        loop(0, rows, step)

    stand_in(0)
    for i in range(STAGES):
        erode_step(i)
        delta_step(i)

    def add_up(row, sums):
        sum_a, sum_b, sum_c, sum_d = sums
        skel_pred, skel_target = skel[0, row], skel[1, row]
        return (
            sum_a + skel_pred * vol[0, 1, XO + row, YE : YE + cols],
            sum_b + skel_pred,
            sum_c + skel_target * vol[0, 0, XO + row, YE : YE + cols],
            sum_d + skel_target,
        )

    sums = lax.fori_loop(0, rows, add_up, (jnp.zeros((cols, planes), jnp.float32),) * 4)
    part[...] = jnp.zeros_like(part)
    for k in range(4):
        part[k : k + 1] = jnp.sum(sums[k], axis=0, keepdims=True)

    slots_y[gy] = part[...]
    copies_y = []
    for k in range(1, ngy):
        copy = pltpu.make_async_remote_copy(
            src_ref=part, dst_ref=slots_y.at[gy], send_sem=sy_send.at[k], recv_sem=sy_recv.at[k],
            device_id=(gx, lax.rem(gy + k, ngy)), device_id_type=MESH,
        )
        copy.start()
        copies_y.append(copy)

    def split(total, low, mid, high, first, sign):
        to_high = share(high, first) if sign > 0 else share(first, high)
        to_low = share(low, mid) if sign > 0 else share(mid, low)
        high_part = total * to_high
        rest = total - high_part
        low_part = rest * to_low
        return low_part, high_part, rest - low_part

    def dilate_weights(row):
        for i in range(STAGES):
            low, mid, high = [vol[i + 1, 0, XO + row + x, 4 : 4 + span] for x in (-1, 0, 1)]
            first = jnp.maximum(low, mid)
            to_low, to_high, to_mid = split(1.0, low, mid, high, first, -1)
            wx[i, LO, XO + row] = to_low
            wx[i, UP, XO + row] = to_high
            wx[i, MID, XO + row] = to_mid
            pool[i, row] = jnp.maximum(first, high)

    loop(0, rows, dilate_weights, 1)

    def dilate_weights_2(row):
        below = 1.0
        for i in reversed(range(STAGES)):
            low, mid, high = [pool[i, row, 4 + y : 4 + y + cols] for y in (-1, 0, 1)]
            first = jnp.maximum(low, mid)
            to_low, to_high, to_mid = split(1.0, low, mid, high, first, -1)
            wy[i, LO, row, YW : YW + cols] = to_low
            wy[i, UP, row, YW : YW + cols] = to_high
            wy[i, MID, row, YW : YW + cols] = to_mid
            mid = jnp.maximum(first, high)
            low, high = before(mid, -jnp.inf), after(mid)
            first = jnp.maximum(low, mid)
            to_low, to_high, to_mid = split(1.0, low, mid, high, first, -1)
            wz[i, LO, row] = to_low
            wz[i, UP, row] = jnp.where(at_last, 0.0, to_high)
            wz[i, MID, row] = jnp.where(at_last, to_high + to_mid, to_mid)
            delta = dels[i, row]
            if i > 0:
                old = befores[i, row]
                passed = jnp.where(delta - old * delta > 0.0, below, 0.0)
                coefs[i, row] = passed - passed * old
                below = below - passed * delta
            else:
                coefs[i, row] = jnp.where(delta > 0.0, below, 0.0)

    loop(0, rows, dilate_weights_2, 1)

    @pl.when(gy == 0)
    def _():
        edge = pl.ds(YW, 1)
        for i in range(STAGES):
            wy[i, MID, :, edge] = wy[i, MID, :, edge] + wy[i, LO, :, edge]
            wy[i, LO, :, edge] = jnp.zeros((rows, 1, planes), jnp.float32)

    @pl.when(gy == ngy - 1)
    def _():
        edge = pl.ds(YW + cols - 1, 1)
        for i in range(STAGES):
            wy[i, MID, :, edge] = wy[i, MID, :, edge] + wy[i, UP, :, edge]
            wy[i, UP, :, edge] = jnp.zeros((rows, 1, planes), jnp.float32)

    @pl.when(gx == 0)
    def _():
        for i in range(STAGES):
            wx[i, MID, XO] = wx[i, MID, XO] + wx[i, LO, XO]
            wx[i, LO, XO] = jnp.zeros((span, planes), jnp.float32)

    @pl.when(gx == ngx - 1)
    def _():
        edge = XO + rows - 1
        for i in range(STAGES):
            wx[i, MID, edge] = wx[i, MID, edge] + wx[i, UP, edge]
            wx[i, UP, edge] = jnp.zeros((span, planes), jnp.float32)

    def erode_weights(i):
        reach = STAGES - i
        every = pl.ds(XO - reach, rows + 2 * reach)
        mine = slice(8, 8 + span)

        def step(row):
            mid = vol[i, 0, row, 4 : 4 + span]
            x_low, x_high = vol[i, 0, row - 1, 4 : 4 + span], vol[i, 0, row + 1, 4 : 4 + span]
            y_low, y_high = vol[i, 0, row, 3 : 3 + span], vol[i, 0, row, 5 : 5 + span]
            z_low, z_high = before(mid, jnp.inf), after(mid)
            x_first, y_first, z_first = [jnp.minimum(low, mid) for low in (x_low, y_low, z_low)]
            x_pool, y_pool = jnp.minimum(x_first, x_high), jnp.minimum(y_first, y_high)
            z_pool = jnp.minimum(z_first, z_high)
            to_z = share(z_pool, jnp.minimum(x_pool, y_pool))
            rest = 1.0 - to_z
            to_y = rest * share(y_pool, x_pool)
            x_parts = split(rest - to_y, x_low, mid, x_high, x_first, 1)
            y_parts = split(to_y, y_low, mid, y_high, y_first, 1)
            z_parts = split(to_z, z_low, mid, z_high, z_first, 1)
            wgt[i, XL, row, mine] = x_parts[0]
            wgt[i, XU, row, mine] = x_parts[1]
            wgt[i, YL, row, mine] = y_parts[0]
            wgt[i, YU, row, mine] = y_parts[1]
            wgt[i, ZL, row, mine] = z_parts[0]
            wgt[i, ZU, row, mine] = jnp.where(at_last, 0.0, z_parts[1])
            centre = x_parts[2] + y_parts[2] + z_parts[2]
            wgt[i, CC, row, mine] = jnp.where(at_last, centre + z_parts[1], centre)

        loop(XO - reach, XO + rows + reach, step)

        for there_is_none, edge, kind in ((gy == 0, YW, YL), (gy == ngy - 1, YW + cols - 1, YU)):
            @pl.when(there_is_none)
            def _(edge=pl.ds(edge, 1), kind=kind):
                wgt[i, CC, every, edge] = wgt[i, CC, every, edge] + wgt[i, kind, every, edge]
                wgt[i, kind, every, edge] = jnp.zeros((rows + 2 * reach, 1, planes), jnp.float32)

        for there_is_none, edge, kind in ((gx == 0, XO, XL), (gx == ngx - 1, XO + rows - 1, XU)):
            @pl.when(there_is_none)
            def _(edge=edge, kind=kind):
                wgt[i, CC, edge, mine] = wgt[i, CC, edge, mine] + wgt[i, kind, edge, mine]
                wgt[i, kind, edge, mine] = jnp.zeros((span, planes), jnp.float32)

    erode_weights(0)

    for copy in copies_y:
        copy.wait()
    total = slots_y[0]
    for k in range(1, ngy):
        total = total + slots_y[k]
    part[...] = total
    slots_x[gx] = total
    copies_x = []
    for k in range(1, ngx):
        copy = pltpu.make_async_remote_copy(
            src_ref=part, dst_ref=slots_x.at[gx], send_sem=sx_send.at[k], recv_sem=sx_recv.at[k],
            device_id=(lax.rem(gx + k, ngx), gy), device_id_type=MESH,
        )
        copy.start()
        copies_x.append(copy)

    for i in range(1, STAGES):
        erode_weights(i)

    for copy in copies_x:
        copy.wait()
    total = slots_x[0]
    for k in range(1, ngx):
        total = total + slots_x[k]
    sum_a, sum_b, sum_c, sum_d = [jnp.sum(total[k : k + 1], axis=1, keepdims=True) for k in range(4)]
    precision = (sum_a + 1.0) / (sum_b + 1.0)
    sensitivity = (sum_c + 1.0) / (sum_d + 1.0)
    together = precision + sensitivity
    loss[...] = 1.0 - 2.0 * precision * sensitivity / together
    cells = float(rows * ngx * cols * ngy * planes)
    coef_pred = cells * (-2.0 * sensitivity * sensitivity / (together * together)) / (sum_b + 1.0)
    coef_target = cells * (-2.0 * precision * precision / (together * together)) / (sum_d + 1.0)
    precision, coef_pred, coef_target = [
        jnp.broadcast_to(value, (cols, planes)) for value in (precision, coef_pred, coef_target)
    ]

    def start_back(row):
        cotangent = coef_pred * (vol[0, 1, XO + row, YE : YE + cols] - precision)
        for i in range(STAGES):
            given = cotangent * coefs[i, row]
            grad[i, XO + row, YW : YW + cols] = given
            hz[i, row, YW : YW + cols] = -(
                given * wz[i, MID, row]
                + pltpu.roll(given * wz[i, LO, row], planes - 1, 1)
                + pltpu.roll(given * wz[i, UP, row], 1, 1)
            )

    loop(0, rows, start_back, 1)

    def back_columns(row):
        for i in range(STAGES):
            hy[i, XO + row] = (
                wy[i, MID, row, 8 : 8 + span] * hz[i, row, 8 : 8 + span]
                + wy[i, LO, row, 9 : 9 + span] * hz[i, row, 9 : 9 + span]
                + wy[i, UP, row, 7 : 7 + span] * hz[i, row, 7 : 7 + span]
            )

    loop(0, rows, back_columns, 1)

    def back_rows(row):
        for i in range(STAGES):
            grad[i + 1, row, 8 : 8 + span] = grad[i + 1, row, 8 : 8 + span] + (
                wx[i, MID, row] * hy[i, row]
                + wx[i, LO, row + 1] * hy[i, row + 1]
                + wx[i, UP, row - 1] * hy[i, row - 1]
            )

    loop(XO - 1, XO + rows + 1, back_rows, 1)

    def gather(i, row, low, length):
        here = slice(low, low + length)
        up, down = slice(low + 1, low + 1 + length), slice(low - 1, low - 1 + length)
        value = grad[i + 1, row, here]
        return (
            grad[i, row, here]
            + wgt[i, CC, row, here] * value
            + wgt[i, XL, row + 1, here] * grad[i + 1, row + 1, here]
            + wgt[i, XU, row - 1, here] * grad[i + 1, row - 1, here]
            + wgt[i, YL, row, up] * grad[i + 1, row, up]
            + wgt[i, YU, row, down] * grad[i + 1, row, down]
            + pltpu.roll(wgt[i, ZL, row, here] * value, planes - 1, 1)
            + pltpu.roll(wgt[i, ZU, row, here] * value, 1, 1)
        )

    for i in reversed(range(1, STAGES)):
        def step(row, i=i):
            grad[i, row, 8 : 8 + span] = gather(i, row, 8, span)

        loop(XO - DEPTH + i, XO + rows + DEPTH - i, step)

    def last_step(row):
        final[row] = gather(0, row, YW - 8, cols + 16)

    loop(XO - DEPTH, XO + rows + DEPTH, last_step)

    returns = []
    for k, (dx, dy) in enumerate(DIRS):
        if dx and dy:
            place = got_c.at[k - 4]
        elif dx:
            place = got_x.at[k]
        else:
            place = got_y.at[k - 2]
        copy = pltpu.make_async_remote_copy(
            src_ref=final.at[strip(dx, rows, XO, DEPTH, True), strip(dy, cols, YE, 8, True)],
            dst_ref=place,
            send_sem=g_send.at[k],
            recv_sem=g_recv.at[k],
            device_id=(gx + dx, gy + dy),
            device_id_type=MESH,
        )
        returns.append((copy, place))
        pl.when(there(dx, dy))(copy.start)

    def finish(row):
        out[row] = final[XO + row, YE : YE + cols] + coef_target * skel[1, row]

    loop(0, rows, finish)

    for k, (dx, dy) in enumerate(DIRS):
        copy, place = returns[k]

        @pl.when(there(-dx, -dy))
        def _(copy=copy, place=place, dx=dx, dy=dy):
            copy.wait_recv()
            at = (strip(-dx, rows, 0, DEPTH, False), strip(-dy, cols, 0, 8, False))
            out[at] = out[at] + place[...]

    for k, (dx, dy) in enumerate(DIRS):
        @pl.when(there(dx, dy))
        def _(k=k):
            halos[k].wait_send()
            returns[k][0].wait_send()


def body(prediction, label_mask, confidence):
    rows, cols, planes = prediction.shape
    ngx, ngy = lax.axis_size("gx"), lax.axis_size("gy")
    f32 = jnp.float32
    wide = rows + 2 * XO
    dma = pltpu.SemaphoreType.DMA
    gradient, loss = pl.pallas_call(
        functools.partial(kernel, (rows, cols, planes, ngx, ngy)),
        out_shape=(jax.ShapeDtypeStruct((rows, cols, planes), f32), jax.ShapeDtypeStruct((1, 1), f32)),
        in_specs=[pl.BlockSpec(memory_space=pl.ANY)] * 3,
        out_specs=(pl.BlockSpec(memory_space=pltpu.VMEM), pl.BlockSpec(memory_space=pltpu.VMEM)),
        scratch_shapes=[
            pltpu.VMEM((STAGES + 1, 2, wide, cols + 16, planes), f32),
            pltpu.VMEM((rows, cols, planes), jnp.int32),
            pltpu.VMEM((rows, cols, planes), f32),
            pltpu.VMEM((2, rows, cols, planes), f32),
            pltpu.VMEM((STAGES, rows, cols, planes), f32),
            pltpu.VMEM((STAGES, rows, cols, planes), f32),
            pltpu.VMEM((STAGES, rows, cols, planes), f32),
            pltpu.VMEM((STAGES, rows, cols + 8, planes), f32),
            pltpu.VMEM((STAGES, 7, wide, cols + 24, planes), f32),
            pltpu.VMEM((STAGES, 3, wide, cols + 8, planes), f32),
            pltpu.VMEM((STAGES, 3, rows, cols + 24, planes), f32),
            pltpu.VMEM((STAGES, 3, rows, cols, planes), f32),
            pltpu.VMEM((STAGES + 1, wide, cols + 24, planes), f32),
            pltpu.VMEM((STAGES, rows, cols + 24, planes), f32),
            pltpu.VMEM((STAGES, wide, cols + 8, planes), f32),
            pltpu.VMEM((wide, cols + 16, planes), f32),
            pltpu.VMEM((8, planes), f32),
            pltpu.VMEM((ngy, 8, planes), f32),
            pltpu.VMEM((ngx, 8, planes), f32),
            pltpu.VMEM((2, DEPTH, cols, planes), f32),
            pltpu.VMEM((2, rows, 8, planes), f32),
            pltpu.VMEM((4, DEPTH, 8, planes), f32),
            dma((3,)),
            dma((8,)),
            dma((8,)),
            dma((ngy,)),
            dma((ngy,)),
            dma((ngx,)),
            dma((ngx,)),
            dma((8,)),
            dma((8,)),
        ],
        compiler_params=pltpu.CompilerParams(
            collective_id=0, has_side_effects=True, vmem_limit_bytes=60 * 1024 * 1024
        ),
    )(prediction, label_mask, confidence)
    return gradient, loss[0, 0]


def solution(mesh):
    placed = (P("gx", "gy", None), P("gx", "gy", None), P("gx", "gy", None))
    return jax.shard_map(
        body, mesh=mesh, in_specs=placed, out_specs=(P("gx", "gy", None), P()), check_vma=False
    )
```

```python
import functools

import jax
import jax.numpy as jnp
from jax import lax
from jax.experimental import pallas as pl
from jax.experimental.pallas import tpu as pltpu
from jax.sharding import PartitionSpec as P

ITERS = 3
STAGES = ITERS + 1
DEPTH = ITERS + 2
XO = 8
YE = 8
YW = 12
MESH = pl.DeviceIdType.MESH
XL, XU, YL, YU, ZL, ZU, CC = range(7)
LO, UP, MID = range(3)
DIRS = ((-1, 0), (1, 0), (0, -1), (0, 1), (-1, -1), (-1, 1), (1, -1), (1, 1))


def share(winner, other):
    return jnp.where(winner < other, 1.0, jnp.where(winner == other, 0.5, 0.0))


def loop(low, high, body, step=4):
    count = (high - low) // step

    if count == 1:
        for row in range(low, low + step):
            body(row)
    else:

        @pl.loop(0, count)
        def _(index):
            for k in range(step):
                body(low + index * step + k)

    for row in range(low + count * step, high):
        body(row)


def halves(*parts):
    @pl.loop(0, 2)
    def _(index):
        for low, high, body in parts:
            step = (high - low) // 2
            for k in range(step):
                body(low + index * step + k)

    for low, high, body in parts:
        if (high - low) % 2:
            body(high - 1)


def kernel(
    sizes, pred_hbm, label_hbm, conf_hbm, out, loss,
    vol, lab, conf, skel, dels, coefs, pool, wgt, wx, wy, wz, base, grad, hz, hy, final,
    part, slots_y, slots_x, got_x, got_y, got_c,
    in_sem, halo_send, halo_recv, sy_send, sy_recv, sx_send, sx_recv, g_send, g_recv,
):
    rows, cols, planes, ngx, ngy = sizes
    gx, gy = lax.axis_index("gx"), lax.axis_index("gy")
    own_x, own_y, own_w = pl.ds(XO, rows), pl.ds(YE, cols), pl.ds(YW, cols)
    span = cols + 8
    lanes = lax.broadcasted_iota(jnp.int32, (1, planes), 1)
    at_first, at_last = lanes == 0, lanes == planes - 1

    loads = [
        pltpu.make_async_copy(pred_hbm, vol[0].at[0, own_x, own_y], in_sem.at[0]),
        pltpu.make_async_copy(label_hbm, lab, in_sem.at[1]),
        pltpu.make_async_copy(conf_hbm, conf, in_sem.at[2]),
    ]
    for copy in loads:
        copy.start()

    def there(dx, dy):
        found = None
        for d, me, size in ((dx, gx, ngx), (dy, gy, ngy)):
            if d:
                inside = (me > 0) if d < 0 else (me < size - 1)
                found = inside if found is None else jnp.logical_and(found, inside)
        return found

    barrier = pltpu.get_barrier_semaphore()
    for k in range(1, ngx):
        pl.semaphore_signal(barrier, inc=1, device_id=(lax.rem(gx + k, ngx), gy), device_id_type=MESH)
    for k in range(1, ngy):
        pl.semaphore_signal(barrier, inc=1, device_id=(gx, lax.rem(gy + k, ngy)), device_id_type=MESH)
    for dx, dy in DIRS[4:]:
        @pl.when(there(dx, dy))
        def _(dx=dx, dy=dy):
            pl.semaphore_signal(barrier, inc=1, device_id=(gx + dx, gy + dy), device_id_type=MESH)

    for copy in loads:
        copy.wait()

    def make_target(row):
        vol[0][1, XO + row, YE : YE + cols] = lab[row].astype(jnp.float32) * conf[row]

    loop(0, rows, make_target)

    corners = 1
    for me, size in ((gx, ngx), (gy, ngy)):
        corners *= lax.div(me + size - 1, size) + lax.div(2 * size - 2 - me, size)
    pl.semaphore_wait(barrier, ngx - 1 + ngy - 1 + corners)

    def strip(d, length, offset, width, outside):
        if d == 0:
            return pl.ds(offset, length)
        if d < 0:
            return pl.ds(offset - width if outside else offset, width)
        return pl.ds(offset + length if outside else offset + length - width, width)

    halos = []
    for k, (dx, dy) in enumerate(DIRS):
        copy = pltpu.make_async_remote_copy(
            src_ref=vol[0].at[:, strip(dx, rows, XO, DEPTH, False), strip(dy, cols, YE, 8, False)],
            dst_ref=vol[0].at[:, strip(-dx, rows, XO, DEPTH, True), strip(-dy, cols, YE, 8, True)],
            send_sem=halo_send.at[k],
            recv_sem=halo_recv.at[k],
            device_id=(gx + dx, gy + dy),
            device_id_type=MESH,
        )
        halos.append(copy)
        pl.when(there(dx, dy))(copy.start)

    def clear_grad(row):
        for i in range(STAGES + 1):
            base[i][row] = jnp.zeros((cols + 24, planes), jnp.float32)
            if 0 < i < STAGES:
                grad[i][row] = jnp.zeros((cols + 24, planes), jnp.float32)

    loop(XO - DEPTH - 1, XO + rows + DEPTH + 1, clear_grad)
    for i in range(STAGES):
        reach = STAGES - i
        for row in (XO - reach - 2, XO - reach - 1, XO + rows + reach, XO + rows + reach + 1):
            for kind in range(7):
                wgt[i, kind, row] = jnp.zeros((cols + 24, planes), jnp.float32)
        for row in (XO - 2, XO - 1, XO + rows, XO + rows + 1):
            hy[i, row] = jnp.zeros((span, planes), jnp.float32)
            for kind in range(3):
                wx[i, kind, row] = jnp.zeros((span, planes), jnp.float32)

    tile = jnp.zeros((8, planes), jnp.float32)

    def clear_sides(row):
        for i in range(STAGES):
            for kind in range(7):
                if i == 0 or kind == YU:
                    wgt[i, kind, row, 0:8] = tile
                if i == 0 or kind == YL:
                    wgt[i, kind, row, cols + 16 : cols + 24] = tile

    loop(XO - STAGES, XO + rows + STAGES, clear_sides)

    def clear_pools(row):
        for i in range(STAGES):
            hz[i, row, YW - 8 : YW] = tile
            hz[i, row, YW + cols : YW + cols + 8] = tile
            for kind in range(3):
                wy[i, kind, row, YW - 8 : YW] = tile
                wy[i, kind, row, YW + cols : YW + cols + 8] = tile

    loop(0, rows, clear_pools)

    for k, (dx, dy) in enumerate(DIRS):
        pl.when(there(-dx, -dy))(halos[k].wait_recv)

    def stand_in(i):
        reach = DEPTH - i
        every = pl.ds(XO - reach, rows + 2 * reach)

        @pl.when(gy == 0)
        def _():
            vol[i][:, every, YE - 1 : YE] = vol[i][:, every, YE : YE + 1]

        @pl.when(gy == ngy - 1)
        def _():
            vol[i][:, every, YE + cols : YE + cols + 1] = vol[i][:, every, YE + cols - 1 : YE + cols]

        @pl.when(gx == 0)
        def _():
            vol[i][:, XO - 1] = vol[i][:, XO]

        @pl.when(gx == ngx - 1)
        def _():
            vol[i][:, XO + rows] = vol[i][:, XO + rows - 1]

    def before(value, edge):
        return jnp.where(at_first, edge, pltpu.roll(value, 1, 1))

    def after(value):
        return jnp.where(at_last, value, pltpu.roll(value, planes - 1, 1))

    def erode_step(i):
        reach = STAGES - i

        def step(row):
            for v in range(2):
                mid = vol[i][v, row, 4 : 4 + span]
                least = jnp.minimum(vol[i][v, row - 1, 4 : 4 + span], vol[i][v, row + 1, 4 : 4 + span])
                sides = jnp.minimum(vol[i][v, row, 3 : 3 + span], vol[i][v, row, 5 : 5 + span])
                along = jnp.minimum(before(mid, mid), after(mid))
                vol[i + 1][v, row, 4 : 4 + span] = jnp.minimum(jnp.minimum(least, sides), jnp.minimum(along, mid))

        return XO - reach, XO + rows + reach, step

    def delta_step(i):
        def step(row):
            for v in range(2):
                most = None
                for x in (-1, 0, 1):
                    for y in (-1, 0, 1):
                        value = vol[i + 1][v, XO + row + x, YE + y : YE + y + cols]
                        most = value if most is None else jnp.maximum(most, value)
                most = jnp.maximum(jnp.maximum(before(most, most), most), after(most))
                delta = jnp.maximum(vol[i][v, XO + row, YE : YE + cols] - most, 0.0)
                if i == 0:
                    result = delta
                else:
                    old = skel[i - 1][v, row]
                    result = old + jnp.maximum(delta - old * delta, 0.0)
                skel[i][v, row] = result
                if v == 0:
                    dels[i, row] = delta

        return 0, rows, step

    stand_in(0)
    halves(erode_step(0))
    stand_in(1)
    for i in range(1, STAGES):
        halves(delta_step(i - 1), erode_step(i))
        stand_in(i + 1)
    halves(delta_step(STAGES - 1))

    def add_up(row, sums):
        sum_a, sum_b, sum_c, sum_d = sums
        skel_pred, skel_target = skel[ITERS][0, row], skel[ITERS][1, row]
        return (
            sum_a + skel_pred * vol[0][1, XO + row, YE : YE + cols],
            sum_b + skel_pred,
            sum_c + skel_target * vol[0][0, XO + row, YE : YE + cols],
            sum_d + skel_target,
        )

    sums = (jnp.zeros((cols, planes), jnp.float32),) * 4
    for row in range(rows):
        sums = add_up(row, sums)
    part[...] = jnp.zeros_like(part)
    for k in range(4):
        part[k : k + 1] = jnp.sum(sums[k], axis=0, keepdims=True)

    slots_y[gy] = part[...]
    copies_y = []
    for k in range(1, ngy):
        copy = pltpu.make_async_remote_copy(
            src_ref=part, dst_ref=slots_y.at[gy], send_sem=sy_send.at[k], recv_sem=sy_recv.at[k],
            device_id=(gx, lax.rem(gy + k, ngy)), device_id_type=MESH,
        )
        copy.start()
        copies_y.append(copy)

    def split(total, low, mid, high, first, sign):
        to_high = share(high, first) if sign > 0 else share(first, high)
        to_low = share(low, mid) if sign > 0 else share(mid, low)
        high_part = total * to_high
        rest = total - high_part
        low_part = rest * to_low
        return low_part, high_part, rest - low_part

    def dilate_weights(row):
        for i in range(STAGES):
            low, mid, high = [vol[i + 1][0, XO + row + x, 4 : 4 + span] for x in (-1, 0, 1)]
            first = jnp.maximum(low, mid)
            to_low, to_high, to_mid = split(1.0, low, mid, high, first, -1)
            wx[i, LO, XO + row] = to_low
            wx[i, UP, XO + row] = to_high
            wx[i, MID, XO + row] = to_mid
            pool[i, row] = jnp.maximum(first, high)

    loop(0, rows, dilate_weights, 2)

    def dilate_weights_2(row):
        below = 1.0
        for i in reversed(range(STAGES)):
            low, mid, high = [pool[i, row, 4 + y : 4 + y + cols] for y in (-1, 0, 1)]
            first = jnp.maximum(low, mid)
            to_low, to_high, to_mid = split(1.0, low, mid, high, first, -1)
            wy[i, LO, row, YW : YW + cols] = to_low
            wy[i, UP, row, YW : YW + cols] = to_high
            wy[i, MID, row, YW : YW + cols] = to_mid
            mid = jnp.maximum(first, high)
            low, high = before(mid, -jnp.inf), after(mid)
            first = jnp.maximum(low, mid)
            to_low, to_high, to_mid = split(1.0, low, mid, high, first, -1)
            wz[i, LO, row] = to_low
            wz[i, UP, row] = jnp.where(at_last, 0.0, to_high)
            wz[i, MID, row] = jnp.where(at_last, to_high + to_mid, to_mid)
            delta = dels[i, row]
            if i > 0:
                old = skel[i - 1][0, row]
                passed = jnp.where(delta - old * delta > 0.0, below, 0.0)
                coefs[i, row] = passed - passed * old
                below = below - passed * delta
            else:
                coefs[i, row] = jnp.where(delta > 0.0, below, 0.0)

    loop(0, rows, dilate_weights_2, 2)

    @pl.when(gy == 0)
    def _():
        edge = pl.ds(YW, 1)
        for i in range(STAGES):
            wy[i, MID, :, edge] = wy[i, MID, :, edge] + wy[i, LO, :, edge]
            wy[i, LO, :, edge] = jnp.zeros((rows, 1, planes), jnp.float32)

    @pl.when(gy == ngy - 1)
    def _():
        edge = pl.ds(YW + cols - 1, 1)
        for i in range(STAGES):
            wy[i, MID, :, edge] = wy[i, MID, :, edge] + wy[i, UP, :, edge]
            wy[i, UP, :, edge] = jnp.zeros((rows, 1, planes), jnp.float32)

    @pl.when(gx == 0)
    def _():
        for i in range(STAGES):
            wx[i, MID, XO] = wx[i, MID, XO] + wx[i, LO, XO]
            wx[i, LO, XO] = jnp.zeros((span, planes), jnp.float32)

    @pl.when(gx == ngx - 1)
    def _():
        edge = XO + rows - 1
        for i in range(STAGES):
            wx[i, MID, edge] = wx[i, MID, edge] + wx[i, UP, edge]
            wx[i, UP, edge] = jnp.zeros((span, planes), jnp.float32)

    def erode_weights(i):
        reach = STAGES - i
        every = pl.ds(XO - reach, rows + 2 * reach)
        mine = slice(8, 8 + span)

        def step(row):
            mid = vol[i][0, row, 4 : 4 + span]
            x_low, x_high = vol[i][0, row - 1, 4 : 4 + span], vol[i][0, row + 1, 4 : 4 + span]
            y_low, y_high = vol[i][0, row, 3 : 3 + span], vol[i][0, row, 5 : 5 + span]
            z_low, z_high = before(mid, jnp.inf), after(mid)
            x_first, y_first, z_first = [jnp.minimum(low, mid) for low in (x_low, y_low, z_low)]
            x_pool, y_pool = jnp.minimum(x_first, x_high), jnp.minimum(y_first, y_high)
            z_pool = jnp.minimum(z_first, z_high)
            to_z = share(z_pool, jnp.minimum(x_pool, y_pool))
            rest = 1.0 - to_z
            to_y = rest * share(y_pool, x_pool)
            x_parts = split(rest - to_y, x_low, mid, x_high, x_first, 1)
            y_parts = split(to_y, y_low, mid, y_high, y_first, 1)
            z_parts = split(to_z, z_low, mid, z_high, z_first, 1)
            wgt[i, XL, row, mine] = x_parts[0]
            wgt[i, XU, row, mine] = x_parts[1]
            wgt[i, YL, row, mine] = y_parts[0]
            wgt[i, YU, row, mine] = y_parts[1]
            wgt[i, ZL, row, mine] = z_parts[0]
            wgt[i, ZU, row, mine] = jnp.where(at_last, 0.0, z_parts[1])
            centre = x_parts[2] + y_parts[2] + z_parts[2]
            wgt[i, CC, row, mine] = jnp.where(at_last, centre + z_parts[1], centre)

        loop(XO - reach, XO + rows + reach, step)

        for there_is_none, edge, kind in ((gy == 0, YW, YL), (gy == ngy - 1, YW + cols - 1, YU)):
            @pl.when(there_is_none)
            def _(edge=pl.ds(edge, 1), kind=kind):
                wgt[i, CC, every, edge] = wgt[i, CC, every, edge] + wgt[i, kind, every, edge]
                wgt[i, kind, every, edge] = jnp.zeros((rows + 2 * reach, 1, planes), jnp.float32)

        for there_is_none, edge, kind in ((gx == 0, XO, XL), (gx == ngx - 1, XO + rows - 1, XU)):
            @pl.when(there_is_none)
            def _(edge=edge, kind=kind):
                wgt[i, CC, edge, mine] = wgt[i, CC, edge, mine] + wgt[i, kind, edge, mine]
                wgt[i, kind, edge, mine] = jnp.zeros((span, planes), jnp.float32)

    erode_weights(0)

    for copy in copies_y:
        copy.wait()
    total = slots_y[0]
    for k in range(1, ngy):
        total = total + slots_y[k]
    part[...] = total
    slots_x[gx] = total
    copies_x = []
    for k in range(1, ngx):
        copy = pltpu.make_async_remote_copy(
            src_ref=part, dst_ref=slots_x.at[gx], send_sem=sx_send.at[k], recv_sem=sx_recv.at[k],
            device_id=(lax.rem(gx + k, ngx), gy), device_id_type=MESH,
        )
        copy.start()
        copies_x.append(copy)

    for i in range(1, STAGES):
        erode_weights(i)

    for copy in copies_x:
        copy.wait()
    total = slots_x[0]
    for k in range(1, ngx):
        total = total + slots_x[k]
    sum_a, sum_b, sum_c, sum_d = [jnp.sum(total[k : k + 1], axis=1, keepdims=True) for k in range(4)]
    precision = (sum_a + 1.0) / (sum_b + 1.0)
    sensitivity = (sum_c + 1.0) / (sum_d + 1.0)
    together = precision + sensitivity
    loss[...] = 1.0 - 2.0 * precision * sensitivity / together
    cells = float(rows * ngx * cols * ngy * planes)
    coef_pred = cells * (-2.0 * sensitivity * sensitivity / (together * together)) / (sum_b + 1.0)
    coef_target = cells * (-2.0 * precision * precision / (together * together)) / (sum_d + 1.0)
    precision, coef_pred, coef_target = [
        jnp.broadcast_to(value, (cols, planes)) for value in (precision, coef_pred, coef_target)
    ]

    def start_back(row):
        cotangent = coef_pred * (vol[0][1, XO + row, YE : YE + cols] - precision)
        for i in range(STAGES):
            given = cotangent * coefs[i, row]
            base[i][XO + row, YW : YW + cols] = given
            hz[i, row, YW : YW + cols] = -(
                given * wz[i, MID, row]
                + pltpu.roll(given * wz[i, LO, row], planes - 1, 1)
                + pltpu.roll(given * wz[i, UP, row], 1, 1)
            )

    loop(0, rows, start_back, 4)

    def back_columns(row):
        for i in range(STAGES):
            hy[i, XO + row] = (
                wy[i, MID, row, 8 : 8 + span] * hz[i, row, 8 : 8 + span]
                + wy[i, LO, row, 9 : 9 + span] * hz[i, row, 9 : 9 + span]
                + wy[i, UP, row, 7 : 7 + span] * hz[i, row, 7 : 7 + span]
            )

    loop(0, rows, back_columns, 4)

    def back_rows(row):
        for i in range(STAGES):
            base[i + 1][row, 8 : 8 + span] = base[i + 1][row, 8 : 8 + span] + (
                wx[i, MID, row] * hy[i, row]
                + wx[i, LO, row + 1] * hy[i, row + 1]
                + wx[i, UP, row - 1] * hy[i, row - 1]
            )

    halves((XO - 1, XO + rows + 1, back_rows))

    def gather(i, row, low, length):
        source = grad[i + 1] if i + 1 < STAGES else base[i + 1]
        here = slice(low, low + length)
        up, down = slice(low + 1, low + 1 + length), slice(low - 1, low - 1 + length)
        value = source[row, here]
        return (
            base[i][row, here]
            + wgt[i, CC, row, here] * value
            + wgt[i, XL, row + 1, here] * source[row + 1, here]
            + wgt[i, XU, row - 1, here] * source[row - 1, here]
            + wgt[i, YL, row, up] * source[row, up]
            + wgt[i, YU, row, down] * source[row, down]
            + pltpu.roll(wgt[i, ZL, row, here] * value, planes - 1, 1)
            + pltpu.roll(wgt[i, ZU, row, here] * value, 1, 1)
        )

    for i in reversed(range(1, STAGES)):
        def step(row, i=i):
            grad[i][row, 8 : 8 + span] = gather(i, row, 8, span)

        halves((XO - DEPTH + i, XO + rows + DEPTH - i, step))

    def last_step(row):
        final[row] = gather(0, row, YW - 8, cols + 16)

    halves((XO - DEPTH, XO + rows + DEPTH, last_step))

    returns = []
    for k, (dx, dy) in enumerate(DIRS):
        if dx and dy:
            place = got_c.at[k - 4]
        elif dx:
            place = got_x.at[k]
        else:
            place = got_y.at[k - 2]
        copy = pltpu.make_async_remote_copy(
            src_ref=final.at[strip(dx, rows, XO, DEPTH, True), strip(dy, cols, YE, 8, True)],
            dst_ref=place,
            send_sem=g_send.at[k],
            recv_sem=g_recv.at[k],
            device_id=(gx + dx, gy + dy),
            device_id_type=MESH,
        )
        returns.append((copy, place))
        pl.when(there(dx, dy))(copy.start)

    def finish(row):
        out[row] = final[XO + row, YE : YE + cols] + coef_target * skel[ITERS][1, row]

    loop(0, rows, finish)

    for k, (dx, dy) in enumerate(DIRS):
        copy, place = returns[k]

        @pl.when(there(-dx, -dy))
        def _(copy=copy, place=place, dx=dx, dy=dy):
            copy.wait_recv()
            at = (strip(-dx, rows, 0, DEPTH, False), strip(-dy, cols, 0, 8, False))
            out[at] = out[at] + place[...]

    for k, (dx, dy) in enumerate(DIRS):
        @pl.when(there(dx, dy))
        def _(k=k):
            halos[k].wait_send()
            returns[k][0].wait_send()


def body(prediction, label_mask, confidence):
    rows, cols, planes = prediction.shape
    ngx, ngy = lax.axis_size("gx"), lax.axis_size("gy")
    f32 = jnp.float32
    wide = rows + 2 * XO
    dma = pltpu.SemaphoreType.DMA
    gradient, loss = pl.pallas_call(
        functools.partial(kernel, (rows, cols, planes, ngx, ngy)),
        out_shape=(jax.ShapeDtypeStruct((rows, cols, planes), f32), jax.ShapeDtypeStruct((1, 1), f32)),
        in_specs=[pl.BlockSpec(memory_space=pl.ANY)] * 3,
        out_specs=(pl.BlockSpec(memory_space=pltpu.VMEM), pl.BlockSpec(memory_space=pltpu.VMEM)),
        scratch_shapes=[
            [pltpu.VMEM((2, wide, cols + 16, planes), f32)] * (STAGES + 1),
            pltpu.VMEM((rows, cols, planes), jnp.int32),
            pltpu.VMEM((rows, cols, planes), f32),
            [pltpu.VMEM((2, rows, cols, planes), f32)] * STAGES,
            pltpu.VMEM((STAGES, rows, cols, planes), f32),
            pltpu.VMEM((STAGES, rows, cols, planes), f32),
            pltpu.VMEM((STAGES, rows, cols + 8, planes), f32),
            pltpu.VMEM((STAGES, 7, wide, cols + 24, planes), f32),
            pltpu.VMEM((STAGES, 3, wide, cols + 8, planes), f32),
            pltpu.VMEM((STAGES, 3, rows, cols + 24, planes), f32),
            pltpu.VMEM((STAGES, 3, rows, cols, planes), f32),
            [pltpu.VMEM((wide, cols + 24, planes), f32)] * (STAGES + 1),
            [pltpu.VMEM((wide, cols + 24, planes), f32)] * STAGES,
            pltpu.VMEM((STAGES, rows, cols + 24, planes), f32),
            pltpu.VMEM((STAGES, wide, cols + 8, planes), f32),
            pltpu.VMEM((wide, cols + 16, planes), f32),
            pltpu.VMEM((8, planes), f32),
            pltpu.VMEM((ngy, 8, planes), f32),
            pltpu.VMEM((ngx, 8, planes), f32),
            pltpu.VMEM((2, DEPTH, cols, planes), f32),
            pltpu.VMEM((2, rows, 8, planes), f32),
            pltpu.VMEM((4, DEPTH, 8, planes), f32),
            dma((3,)),
            dma((8,)),
            dma((8,)),
            dma((ngy,)),
            dma((ngy,)),
            dma((ngx,)),
            dma((ngx,)),
            dma((8,)),
            dma((8,)),
        ],
        compiler_params=pltpu.CompilerParams(
            collective_id=0, has_side_effects=True, vmem_limit_bytes=60 * 1024 * 1024
        ),
    )(prediction, label_mask, confidence)
    return gradient, loss[0, 0]


def solution(mesh):
    placed = (P("gx", "gy", None), P("gx", "gy", None), P("gx", "gy", None))
    return jax.shard_map(
        body, mesh=mesh, in_specs=placed, out_specs=(P("gx", "gy", None), P()), check_vma=False
    )
```

```python
import functools

import jax
import jax.numpy as jnp
from jax import lax
from jax.experimental import pallas as pl
from jax.experimental.pallas import tpu as pltpu
from jax.sharding import PartitionSpec as P

ITERS = 3
STAGES = ITERS + 1
DEPTH = ITERS + 2
XO = 8
YE = 8
YW = 12
MESH = pl.DeviceIdType.MESH
XL, XU, YL, YU, ZL, ZU, CC = range(7)
LO, UP, MID = range(3)
DIRS = ((-1, 0), (1, 0), (0, -1), (0, 1), (-1, -1), (-1, 1), (1, -1), (1, 1))


def share(winner, other):
    return jnp.where(winner < other, 1.0, jnp.where(winner == other, 0.5, 0.0))


def loop(low, high, body, step=4):
    count = (high - low) // step

    if count == 1:
        for row in range(low, low + step):
            body(row)
    else:

        @pl.loop(0, count)
        def _(index):
            for k in range(step):
                body(low + index * step + k)

    for row in range(low + count * step, high):
        body(row)


def halves(*parts):
    @pl.loop(0, 2)
    def _(index):
        for low, high, body in parts:
            step = (high - low) // 2
            for k in range(step):
                body(low + index * step + k)

    for low, high, body in parts:
        if (high - low) % 2:
            body(high - 1)


def kernel(
    sizes, pred_hbm, label_hbm, conf_hbm, out, loss,
    vol, lab, conf, skel, dels, coefs, pool, wgt, wx, wy, wz, base, grad, hz, hy, final,
    part, slots_y, slots_x, got_x, got_y, got_c, edge_out, edge_in, back_out,
    in_sem, halo_send, halo_recv, sy_send, sy_recv, sx_send, sx_recv, g_send, g_recv,
):
    rows, cols, planes, ngx, ngy = sizes
    gx, gy = lax.axis_index("gx"), lax.axis_index("gy")
    own_x, own_y, own_w = pl.ds(XO, rows), pl.ds(YE, cols), pl.ds(YW, cols)
    span = cols + 8
    lanes = lax.broadcasted_iota(jnp.int32, (1, planes), 1)
    at_first, at_last = lanes == 0, lanes == planes - 1

    loads = [
        pltpu.make_async_copy(pred_hbm, vol[0].at[0, own_x, own_y], in_sem.at[0]),
        pltpu.make_async_copy(label_hbm, lab, in_sem.at[1]),
        pltpu.make_async_copy(conf_hbm, conf, in_sem.at[2]),
    ]
    for copy in loads:
        copy.start()

    def there(dx, dy):
        found = None
        for d, me, size in ((dx, gx, ngx), (dy, gy, ngy)):
            if d:
                inside = (me > 0) if d < 0 else (me < size - 1)
                found = inside if found is None else jnp.logical_and(found, inside)
        return found

    barrier = pltpu.get_barrier_semaphore()
    for k in range(1, ngx):
        pl.semaphore_signal(barrier, inc=1, device_id=(lax.rem(gx + k, ngx), gy), device_id_type=MESH)
    for k in range(1, ngy):
        pl.semaphore_signal(barrier, inc=1, device_id=(gx, lax.rem(gy + k, ngy)), device_id_type=MESH)
    for dx, dy in DIRS[4:]:
        @pl.when(there(dx, dy))
        def _(dx=dx, dy=dy):
            pl.semaphore_signal(barrier, inc=1, device_id=(gx + dx, gy + dy), device_id_type=MESH)

    corners = 1
    for me, size in ((gx, ngx), (gy, ngy)):
        corners *= lax.div(me + size - 1, size) + lax.div(2 * size - 2 - me, size)
    pl.semaphore_wait(barrier, ngx - 1 + ngy - 1 + corners)

    def strip(d, length, offset, width, outside):
        if d == 0:
            return pl.ds(offset, length)
        if d < 0:
            return pl.ds(offset - width if outside else offset, width)
        return pl.ds(offset + length if outside else offset + length - width, width)

    def corner_strips(dx, dy, outside, x_at, y_at):
        offset, found = 0, []
        for i in range(1, DEPTH + 1):
            width = DEPTH + 1 - i
            if outside:
                row = x_at - i if dx < 0 else x_at + rows + i - 1
                column = y_at - width if dy < 0 else y_at + cols
            else:
                row = x_at + i - 1 if dx < 0 else x_at + rows - i
                column = y_at if dy < 0 else y_at + cols - width
            found.append((offset, width, row, slice(column, column + width)))
            offset += width
        return found

    def send_halo(v):
        copies = []
        for k, (dx, dy) in enumerate(DIRS):
            if dx and dy:
                for offset, width, row, columns in corner_strips(dx, dy, False, XO, YE):
                    edge_out[v, k - 4, offset : offset + width] = vol[0][v, row, columns]
                source, target = edge_out.at[v, k - 4], edge_in.at[v, k - 4]
            else:
                source = vol[0].at[v, strip(dx, rows, XO, DEPTH, False), strip(dy, cols, YE, 8, False)]
                target = vol[0].at[v, strip(-dx, rows, XO, DEPTH, True), strip(-dy, cols, YE, 8, True)]
            copy = pltpu.make_async_remote_copy(
                src_ref=source,
                dst_ref=target,
                send_sem=halo_send.at[8 * v + k],
                recv_sem=halo_recv.at[8 * v + k],
                device_id=(gx + dx, gy + dy),
                device_id_type=MESH,
            )
            copies.append(copy)
            pl.when(there(dx, dy))(copy.start)
        return copies

    def wait_halo(v):
        for k, (dx, dy) in enumerate(DIRS):
            @pl.when(there(-dx, -dy))
            def _(k=k, dx=dx, dy=dy):
                halos[v][k].wait_recv()
                if dx and dy:
                    for offset, width, row, columns in corner_strips(-dx, -dy, True, XO, YE):
                        vol[0][v, row, columns] = edge_in[v, k - 4, offset : offset + width]

    loads[0].wait()
    halos = [send_halo(0)]
    loads[1].wait()
    loads[2].wait()

    def make_target(row):
        vol[0][1, XO + row, YE : YE + cols] = lab[row].astype(jnp.float32) * conf[row]

    loop(0, rows, make_target, 8)
    halos.append(send_halo(1))

    def clear_grad(row):
        for i in range(STAGES + 1):
            base[i][row] = jnp.zeros((cols + 24, planes), jnp.float32)
            if 0 < i < STAGES:
                grad[i][row] = jnp.zeros((cols + 24, planes), jnp.float32)

    loop(XO - DEPTH - 1, XO + rows + DEPTH + 1, clear_grad)
    for i in range(STAGES):
        reach = STAGES - i
        for row in (XO - reach - 2, XO - reach - 1, XO + rows + reach, XO + rows + reach + 1):
            for kind in range(7):
                wgt[i, kind, row] = jnp.zeros((cols + 24, planes), jnp.float32)
        for row in (XO - 2, XO - 1, XO + rows, XO + rows + 1):
            hy[i, row] = jnp.zeros((span, planes), jnp.float32)
            for kind in range(3):
                wx[i, kind, row] = jnp.zeros((span, planes), jnp.float32)

    tile = jnp.zeros((8, planes), jnp.float32)

    def clear_sides(row):
        for i in range(STAGES):
            for kind in range(7):
                if i == 0 or kind == YU:
                    wgt[i, kind, row, 0:8] = tile
                if i == 0 or kind == YL:
                    wgt[i, kind, row, cols + 16 : cols + 24] = tile

    loop(XO - STAGES, XO + rows + STAGES, clear_sides)

    def clear_pools(row):
        for i in range(STAGES):
            hz[i, row, YW - 8 : YW] = tile
            hz[i, row, YW + cols : YW + cols + 8] = tile
            for kind in range(3):
                wy[i, kind, row, YW - 8 : YW] = tile
                wy[i, kind, row, YW + cols : YW + cols + 8] = tile

    loop(0, rows, clear_pools)

    def stand_in(i, v):
        reach = DEPTH - i
        every = pl.ds(XO - reach, rows + 2 * reach)

        @pl.when(gy == 0)
        def _():
            vol[i][v, every, YE - 1 : YE] = vol[i][v, every, YE : YE + 1]

        @pl.when(gy == ngy - 1)
        def _():
            vol[i][v, every, YE + cols : YE + cols + 1] = vol[i][v, every, YE + cols - 1 : YE + cols]

        @pl.when(gx == 0)
        def _():
            vol[i][v, XO - 1] = vol[i][v, XO]

        @pl.when(gx == ngx - 1)
        def _():
            vol[i][v, XO + rows] = vol[i][v, XO + rows - 1]

    def before(value, edge):
        return jnp.where(at_first, edge, pltpu.roll(value, 1, 1))

    def after(value):
        return jnp.where(at_last, value, pltpu.roll(value, planes - 1, 1))

    def erode_step(i, v):
        reach = STAGES - i

        def step(row):
            mid = vol[i][v, row, 4 : 4 + span]
            least = jnp.minimum(vol[i][v, row - 1, 4 : 4 + span], vol[i][v, row + 1, 4 : 4 + span])
            sides = jnp.minimum(vol[i][v, row, 3 : 3 + span], vol[i][v, row, 5 : 5 + span])
            along = jnp.minimum(before(mid, mid), after(mid))
            vol[i + 1][v, row, 4 : 4 + span] = jnp.minimum(jnp.minimum(least, sides), jnp.minimum(along, mid))

        return XO - reach, XO + rows + reach, step

    def delta_step(i, v):
        def step(row):
            most = None
            for x in (-1, 0, 1):
                for y in (-1, 0, 1):
                    value = vol[i + 1][v, XO + row + x, YE + y : YE + y + cols]
                    most = value if most is None else jnp.maximum(most, value)
            most = jnp.maximum(jnp.maximum(before(most, most), most), after(most))
            delta = jnp.maximum(vol[i][v, XO + row, YE : YE + cols] - most, 0.0)
            if i == 0:
                result = delta
            else:
                old = skel[i - 1][v, row]
                result = old + jnp.maximum(delta - old * delta, 0.0)
            skel[i][v, row] = result
            if v == 0:
                dels[i, row] = delta

        return 0, rows, step

    def forward(v):
        wait_halo(v)
        stand_in(0, v)
        halves(erode_step(0, v))
        stand_in(1, v)
        for i in range(1, STAGES):
            halves(delta_step(i - 1, v), erode_step(i, v))
            stand_in(i + 1, v)
        halves(delta_step(STAGES - 1, v))

    forward(0)
    def split(total, low, mid, high, first, sign):
        to_high = share(high, first) if sign > 0 else share(first, high)
        to_low = share(low, mid) if sign > 0 else share(mid, low)
        high_part = total * to_high
        rest = total - high_part
        low_part = rest * to_low
        return low_part, high_part, rest - low_part

    def dilate_weights(row):
        for i in range(STAGES):
            low, mid, high = [vol[i + 1][0, XO + row + x, 4 : 4 + span] for x in (-1, 0, 1)]
            first = jnp.maximum(low, mid)
            to_low, to_high, to_mid = split(1.0, low, mid, high, first, -1)
            wx[i, LO, XO + row] = to_low
            wx[i, UP, XO + row] = to_high
            wx[i, MID, XO + row] = to_mid
            pool[i, row] = jnp.maximum(first, high)

    loop(0, rows, dilate_weights, 2)

    def dilate_weights_2(row):
        below = 1.0
        for i in reversed(range(STAGES)):
            low, mid, high = [pool[i, row, 4 + y : 4 + y + cols] for y in (-1, 0, 1)]
            first = jnp.maximum(low, mid)
            to_low, to_high, to_mid = split(1.0, low, mid, high, first, -1)
            wy[i, LO, row, YW : YW + cols] = to_low
            wy[i, UP, row, YW : YW + cols] = to_high
            wy[i, MID, row, YW : YW + cols] = to_mid
            mid = jnp.maximum(first, high)
            low, high = before(mid, -jnp.inf), after(mid)
            first = jnp.maximum(low, mid)
            to_low, to_high, to_mid = split(1.0, low, mid, high, first, -1)
            wz[i, LO, row] = to_low
            wz[i, UP, row] = jnp.where(at_last, 0.0, to_high)
            wz[i, MID, row] = jnp.where(at_last, to_high + to_mid, to_mid)
            delta = dels[i, row]
            if i > 0:
                old = skel[i - 1][0, row]
                passed = jnp.where(delta - old * delta > 0.0, below, 0.0)
                coefs[i, row] = passed - passed * old
                below = below - passed * delta
            else:
                coefs[i, row] = jnp.where(delta > 0.0, below, 0.0)

    loop(0, rows, dilate_weights_2, 2)

    @pl.when(gy == 0)
    def _():
        edge = pl.ds(YW, 1)
        for i in range(STAGES):
            wy[i, MID, :, edge] = wy[i, MID, :, edge] + wy[i, LO, :, edge]
            wy[i, LO, :, edge] = jnp.zeros((rows, 1, planes), jnp.float32)

    @pl.when(gy == ngy - 1)
    def _():
        edge = pl.ds(YW + cols - 1, 1)
        for i in range(STAGES):
            wy[i, MID, :, edge] = wy[i, MID, :, edge] + wy[i, UP, :, edge]
            wy[i, UP, :, edge] = jnp.zeros((rows, 1, planes), jnp.float32)

    @pl.when(gx == 0)
    def _():
        for i in range(STAGES):
            wx[i, MID, XO] = wx[i, MID, XO] + wx[i, LO, XO]
            wx[i, LO, XO] = jnp.zeros((span, planes), jnp.float32)

    @pl.when(gx == ngx - 1)
    def _():
        edge = XO + rows - 1
        for i in range(STAGES):
            wx[i, MID, edge] = wx[i, MID, edge] + wx[i, UP, edge]
            wx[i, UP, edge] = jnp.zeros((span, planes), jnp.float32)

    forward(1)

    def add_up(row, sums):
        sum_a, sum_b, sum_c, sum_d = sums
        skel_pred, skel_target = skel[ITERS][0, row], skel[ITERS][1, row]
        return (
            sum_a + skel_pred * vol[0][1, XO + row, YE : YE + cols],
            sum_b + skel_pred,
            sum_c + skel_target * vol[0][0, XO + row, YE : YE + cols],
            sum_d + skel_target,
        )

    sums = (jnp.zeros((cols, planes), jnp.float32),) * 4
    for row in range(rows):
        sums = add_up(row, sums)
    part[...] = jnp.zeros_like(part)
    for k in range(4):
        part[k : k + 1] = jnp.sum(sums[k], axis=0, keepdims=True)

    slots_y[gy] = part[...]
    copies_y = []
    for k in range(1, ngy):
        copy = pltpu.make_async_remote_copy(
            src_ref=part, dst_ref=slots_y.at[gy], send_sem=sy_send.at[k], recv_sem=sy_recv.at[k],
            device_id=(gx, lax.rem(gy + k, ngy)), device_id_type=MESH,
        )
        copy.start()
        copies_y.append(copy)

    def erode_weights(i):
        reach = STAGES - i
        every = pl.ds(XO - reach, rows + 2 * reach)
        mine = slice(8, 8 + span)

        def step(row):
            mid = vol[i][0, row, 4 : 4 + span]
            x_low, x_high = vol[i][0, row - 1, 4 : 4 + span], vol[i][0, row + 1, 4 : 4 + span]
            y_low, y_high = vol[i][0, row, 3 : 3 + span], vol[i][0, row, 5 : 5 + span]
            z_low, z_high = before(mid, jnp.inf), after(mid)
            x_first, y_first, z_first = [jnp.minimum(low, mid) for low in (x_low, y_low, z_low)]
            x_pool, y_pool = jnp.minimum(x_first, x_high), jnp.minimum(y_first, y_high)
            z_pool = jnp.minimum(z_first, z_high)
            to_z = share(z_pool, jnp.minimum(x_pool, y_pool))
            rest = 1.0 - to_z
            to_y = rest * share(y_pool, x_pool)
            x_parts = split(rest - to_y, x_low, mid, x_high, x_first, 1)
            y_parts = split(to_y, y_low, mid, y_high, y_first, 1)
            z_parts = split(to_z, z_low, mid, z_high, z_first, 1)
            wgt[i, XL, row, mine] = x_parts[0]
            wgt[i, XU, row, mine] = x_parts[1]
            wgt[i, YL, row, mine] = y_parts[0]
            wgt[i, YU, row, mine] = y_parts[1]
            wgt[i, ZL, row, mine] = z_parts[0]
            wgt[i, ZU, row, mine] = jnp.where(at_last, 0.0, z_parts[1])
            centre = x_parts[2] + y_parts[2] + z_parts[2]
            wgt[i, CC, row, mine] = jnp.where(at_last, centre + z_parts[1], centre)

        loop(XO - reach, XO + rows + reach, step)

        for there_is_none, edge, kind in ((gy == 0, YW, YL), (gy == ngy - 1, YW + cols - 1, YU)):
            @pl.when(there_is_none)
            def _(edge=pl.ds(edge, 1), kind=kind):
                wgt[i, CC, every, edge] = wgt[i, CC, every, edge] + wgt[i, kind, every, edge]
                wgt[i, kind, every, edge] = jnp.zeros((rows + 2 * reach, 1, planes), jnp.float32)

        for there_is_none, edge, kind in ((gx == 0, XO, XL), (gx == ngx - 1, XO + rows - 1, XU)):
            @pl.when(there_is_none)
            def _(edge=edge, kind=kind):
                wgt[i, CC, edge, mine] = wgt[i, CC, edge, mine] + wgt[i, kind, edge, mine]
                wgt[i, kind, edge, mine] = jnp.zeros((span, planes), jnp.float32)

    erode_weights(0)

    for copy in copies_y:
        copy.wait()
    total = slots_y[0]
    for k in range(1, ngy):
        total = total + slots_y[k]
    part[...] = total
    slots_x[gx] = total
    copies_x = []
    for k in range(1, ngx):
        copy = pltpu.make_async_remote_copy(
            src_ref=part, dst_ref=slots_x.at[gx], send_sem=sx_send.at[k], recv_sem=sx_recv.at[k],
            device_id=(lax.rem(gx + k, ngx), gy), device_id_type=MESH,
        )
        copy.start()
        copies_x.append(copy)

    for i in range(1, STAGES):
        erode_weights(i)

    for copy in copies_x:
        copy.wait()
    total = slots_x[0]
    for k in range(1, ngx):
        total = total + slots_x[k]
    sum_a, sum_b, sum_c, sum_d = [jnp.sum(total[k : k + 1], axis=1, keepdims=True) for k in range(4)]
    precision = (sum_a + 1.0) / (sum_b + 1.0)
    sensitivity = (sum_c + 1.0) / (sum_d + 1.0)
    together = precision + sensitivity
    loss[...] = 1.0 - 2.0 * precision * sensitivity / together
    cells = float(rows * ngx * cols * ngy * planes)
    coef_pred = cells * (-2.0 * sensitivity * sensitivity / (together * together)) / (sum_b + 1.0)
    coef_target = cells * (-2.0 * precision * precision / (together * together)) / (sum_d + 1.0)
    precision, coef_pred, coef_target = [
        jnp.broadcast_to(value, (cols, planes)) for value in (precision, coef_pred, coef_target)
    ]

    def start_back(row):
        cotangent = coef_pred * (vol[0][1, XO + row, YE : YE + cols] - precision)
        for i in range(STAGES):
            given = cotangent * coefs[i, row]
            base[i][XO + row, YW : YW + cols] = given
            hz[i, row, YW : YW + cols] = -(
                given * wz[i, MID, row]
                + pltpu.roll(given * wz[i, LO, row], planes - 1, 1)
                + pltpu.roll(given * wz[i, UP, row], 1, 1)
            )

    loop(0, rows, start_back, 4)

    def back_columns(row):
        for i in range(STAGES):
            hy[i, XO + row] = (
                wy[i, MID, row, 8 : 8 + span] * hz[i, row, 8 : 8 + span]
                + wy[i, LO, row, 9 : 9 + span] * hz[i, row, 9 : 9 + span]
                + wy[i, UP, row, 7 : 7 + span] * hz[i, row, 7 : 7 + span]
            )

    loop(0, rows, back_columns, 4)

    def back_rows(row):
        for i in range(STAGES):
            base[i + 1][row, 8 : 8 + span] = base[i + 1][row, 8 : 8 + span] + (
                wx[i, MID, row] * hy[i, row]
                + wx[i, LO, row + 1] * hy[i, row + 1]
                + wx[i, UP, row - 1] * hy[i, row - 1]
            )

    halves((XO - 1, XO + rows + 1, back_rows))

    def gather(i, row, low, length):
        source = grad[i + 1] if i + 1 < STAGES else base[i + 1]
        here = slice(low, low + length)
        up, down = slice(low + 1, low + 1 + length), slice(low - 1, low - 1 + length)
        value = source[row, here]
        return (
            base[i][row, here]
            + wgt[i, CC, row, here] * value
            + wgt[i, XL, row + 1, here] * source[row + 1, here]
            + wgt[i, XU, row - 1, here] * source[row - 1, here]
            + wgt[i, YL, row, up] * source[row, up]
            + wgt[i, YU, row, down] * source[row, down]
            + pltpu.roll(wgt[i, ZL, row, here] * value, planes - 1, 1)
            + pltpu.roll(wgt[i, ZU, row, here] * value, 1, 1)
        )

    for i in reversed(range(1, STAGES)):
        def step(row, i=i):
            grad[i][row, 8 : 8 + span] = gather(i, row, 8, span)

        halves((XO - DEPTH + i, XO + rows + DEPTH - i, step))

    def last_step(row):
        final[row] = gather(0, row, YW - 8, cols + 16)

    def send_back(k):
        dx, dy = DIRS[k]
        if dx and dy:
            for offset, width, row, columns in corner_strips(dx, dy, True, XO, YE):
                back_out[k - 4, offset : offset + width] = final[row, columns]
            source, place = back_out.at[k - 4], got_c.at[k - 4]
        else:
            source = final.at[strip(dx, rows, XO, DEPTH, True), strip(dy, cols, YE, 8, True)]
            place = got_x.at[k] if dx else got_y.at[k - 2]
        copy = pltpu.make_async_remote_copy(
            src_ref=source,
            dst_ref=place,
            send_sem=g_send.at[k],
            recv_sem=g_recv.at[k],
            device_id=(gx + dx, gy + dy),
            device_id_type=MESH,
        )
        pl.when(there(dx, dy))(copy.start)
        return copy

    returns = {}
    for side, low in enumerate((XO - DEPTH, XO + rows)):
        for row in range(low, low + DEPTH):
            last_step(row)
        returns[side] = send_back(side)
    for k in range(4, 8):
        returns[k] = send_back(k)

    def middle_step(row):
        value = gather(0, XO + row, YW - 8, cols + 16)
        final[XO + row] = value
        out[row] = value[8 : 8 + cols] + coef_target * skel[ITERS][1, row]

    halves((0, rows, middle_step))
    for k in (2, 3):
        returns[k] = send_back(k)

    for k, (dx, dy) in enumerate(DIRS):
        @pl.when(there(-dx, -dy))
        def _(k=k, dx=dx, dy=dy):
            returns[k].wait_recv()
            if dx and dy:
                for offset, width, row, columns in corner_strips(-dx, -dy, False, 0, 0):
                    out[row, columns] = out[row, columns] + got_c[k - 4, offset : offset + width]
            else:
                at = (strip(-dx, rows, 0, DEPTH, False), strip(-dy, cols, 0, 8, False))
                out[at] = out[at] + (got_x[k] if dx else got_y[k - 2])

    for k, (dx, dy) in enumerate(DIRS):
        @pl.when(there(dx, dy))
        def _(k=k):
            halos[0][k].wait_send()
            halos[1][k].wait_send()
            returns[k].wait_send()


def body(prediction, label_mask, confidence):
    rows, cols, planes = prediction.shape
    ngx, ngy = lax.axis_size("gx"), lax.axis_size("gy")
    f32 = jnp.float32
    wide = rows + 2 * XO
    corner = (DEPTH * (DEPTH + 1) // 2 + 7) // 8 * 8
    dma = pltpu.SemaphoreType.DMA
    gradient, loss = pl.pallas_call(
        functools.partial(kernel, (rows, cols, planes, ngx, ngy)),
        out_shape=(jax.ShapeDtypeStruct((rows, cols, planes), f32), jax.ShapeDtypeStruct((1, 1), f32)),
        in_specs=[pl.BlockSpec(memory_space=pl.ANY)] * 3,
        out_specs=(pl.BlockSpec(memory_space=pltpu.VMEM), pl.BlockSpec(memory_space=pltpu.VMEM)),
        scratch_shapes=[
            [pltpu.VMEM((2, wide, cols + 16, planes), f32)] * (STAGES + 1),
            pltpu.VMEM((rows, cols, planes), jnp.int32),
            pltpu.VMEM((rows, cols, planes), f32),
            [pltpu.VMEM((2, rows, cols, planes), f32)] * STAGES,
            pltpu.VMEM((STAGES, rows, cols, planes), f32),
            pltpu.VMEM((STAGES, rows, cols, planes), f32),
            pltpu.VMEM((STAGES, rows, cols + 8, planes), f32),
            pltpu.VMEM((STAGES, 7, wide, cols + 24, planes), f32),
            pltpu.VMEM((STAGES, 3, wide, cols + 8, planes), f32),
            pltpu.VMEM((STAGES, 3, rows, cols + 24, planes), f32),
            pltpu.VMEM((STAGES, 3, rows, cols, planes), f32),
            [pltpu.VMEM((wide, cols + 24, planes), f32)] * (STAGES + 1),
            [pltpu.VMEM((wide, cols + 24, planes), f32)] * STAGES,
            pltpu.VMEM((STAGES, rows, cols + 24, planes), f32),
            pltpu.VMEM((STAGES, wide, cols + 8, planes), f32),
            pltpu.VMEM((wide, cols + 16, planes), f32),
            pltpu.VMEM((8, planes), f32),
            pltpu.VMEM((ngy, 8, planes), f32),
            pltpu.VMEM((ngx, 8, planes), f32),
            pltpu.VMEM((2, DEPTH, cols, planes), f32),
            pltpu.VMEM((2, rows, 8, planes), f32),
            pltpu.VMEM((4, corner, planes), f32),
            pltpu.VMEM((2, 4, corner, planes), f32),
            pltpu.VMEM((2, 4, corner, planes), f32),
            pltpu.VMEM((4, corner, planes), f32),
            dma((3,)),
            dma((16,)),
            dma((16,)),
            dma((ngy,)),
            dma((ngy,)),
            dma((ngx,)),
            dma((ngx,)),
            dma((8,)),
            dma((8,)),
        ],
        compiler_params=pltpu.CompilerParams(
            collective_id=0, has_side_effects=True, vmem_limit_bytes=60 * 1024 * 1024
        ),
    )(prediction, label_mask, confidence)
    return gradient, loss[0, 0]


def solution(mesh):
    placed = (P("gx", "gy", None), P("gx", "gy", None), P("gx", "gy", None))
    return jax.shard_map(
        body, mesh=mesh, in_specs=placed, out_specs=(P("gx", "gy", None), P()), check_vma=False
    )
```

```python
import functools

import jax
import jax.numpy as jnp
from jax import lax
from jax.experimental import pallas as pl
from jax.experimental.pallas import tpu as pltpu
from jax.sharding import PartitionSpec as P

ITERS = 3
STAGES = ITERS + 1
DEPTH = ITERS + 2
XO = 8
YE = 8
YW = 12
MESH = pl.DeviceIdType.MESH
XL, XU, YL, YU, ZL, ZU, CC = range(7)
LO, UP, MID = range(3)
DIRS = ((-1, 0), (1, 0), (0, -1), (0, 1), (-1, -1), (-1, 1), (1, -1), (1, 1))


def share(winner, other):
    return jnp.where(winner < other, 1.0, jnp.where(winner == other, 0.5, 0.0))


def loop(low, high, body, step=4):
    count = (high - low) // step

    if count == 1:
        for row in range(low, low + step):
            body(row)
    else:

        @pl.loop(0, count)
        def _(index):
            for k in range(step):
                body(low + index * step + k)

    for row in range(low + count * step, high):
        body(row)


def halves(*parts):
    @pl.loop(0, 2)
    def _(index):
        for low, high, body in parts:
            step = (high - low) // 2
            for k in range(step):
                body(low + index * step + k)

    for low, high, body in parts:
        if (high - low) % 2:
            body(high - 1)


def straight(*parts):
    for low, high, body in parts:
        for row in range(low, high):
            body(row)


def kernel(
    sizes, pred_hbm, label_hbm, conf_hbm, out, loss,
    vol, lab, conf, skel, dels, coefs, pool, wgt, wx, wy, wz, base, grad, hz, hy, final,
    part, slots_y, slots_x, got_x, got_y, got_c, edge_out, edge_in, back_out,
    in_sem, halo_send, halo_recv, sy_send, sy_recv, sx_send, sx_recv, g_send, g_recv,
):
    rows, cols, planes, ngx, ngy = sizes
    gx, gy = lax.axis_index("gx"), lax.axis_index("gy")
    own_x, own_y, own_w = pl.ds(XO, rows), pl.ds(YE, cols), pl.ds(YW, cols)
    span = cols + 8
    lanes = lax.broadcasted_iota(jnp.int32, (1, planes), 1)
    at_first, at_last = lanes == 0, lanes == planes - 1

    loads = [
        pltpu.make_async_copy(pred_hbm, vol[0].at[0, own_x, own_y], in_sem.at[0]),
        pltpu.make_async_copy(label_hbm, lab, in_sem.at[1]),
        pltpu.make_async_copy(conf_hbm, conf, in_sem.at[2]),
    ]
    for copy in loads:
        copy.start()

    def there(dx, dy):
        found = None
        for d, me, size in ((dx, gx, ngx), (dy, gy, ngy)):
            if d:
                inside = (me > 0) if d < 0 else (me < size - 1)
                found = inside if found is None else jnp.logical_and(found, inside)
        return found

    barrier = pltpu.get_barrier_semaphore()
    for k in range(1, ngx):
        pl.semaphore_signal(barrier, inc=1, device_id=(lax.rem(gx + k, ngx), gy), device_id_type=MESH)
    for k in range(1, ngy):
        pl.semaphore_signal(barrier, inc=1, device_id=(gx, lax.rem(gy + k, ngy)), device_id_type=MESH)
    for dx, dy in DIRS[4:]:
        @pl.when(there(dx, dy))
        def _(dx=dx, dy=dy):
            pl.semaphore_signal(barrier, inc=1, device_id=(gx + dx, gy + dy), device_id_type=MESH)

    corners = 1
    for me, size in ((gx, ngx), (gy, ngy)):
        corners *= lax.div(me + size - 1, size) + lax.div(2 * size - 2 - me, size)
    pl.semaphore_wait(barrier, ngx - 1 + ngy - 1 + corners)

    def strip(d, length, offset, width, outside):
        if d == 0:
            return pl.ds(offset, length)
        if d < 0:
            return pl.ds(offset - width if outside else offset, width)
        return pl.ds(offset + length if outside else offset + length - width, width)

    def corner_strips(dx, dy, outside, x_at, y_at):
        offset, found = 0, []
        for i in range(1, DEPTH + 1):
            width = DEPTH + 1 - i
            if outside:
                row = x_at - i if dx < 0 else x_at + rows + i - 1
                column = y_at - width if dy < 0 else y_at + cols
            else:
                row = x_at + i - 1 if dx < 0 else x_at + rows - i
                column = y_at if dy < 0 else y_at + cols - width
            found.append((offset, width, row, slice(column, column + width)))
            offset += width
        return found

    def send_halo(v):
        copies = []
        for k, (dx, dy) in enumerate(DIRS):
            if dx and dy:
                for offset, width, row, columns in corner_strips(dx, dy, False, XO, YE):
                    edge_out[v, k - 4, offset : offset + width] = vol[0][v, row, columns]
                source, target = edge_out.at[v, k - 4], edge_in.at[v, k - 4]
            else:
                source = vol[0].at[v, strip(dx, rows, XO, DEPTH, False), strip(dy, cols, YE, 8, False)]
                target = vol[0].at[v, strip(-dx, rows, XO, DEPTH, True), strip(-dy, cols, YE, 8, True)]
            copy = pltpu.make_async_remote_copy(
                src_ref=source,
                dst_ref=target,
                send_sem=halo_send.at[8 * v + k],
                recv_sem=halo_recv.at[8 * v + k],
                device_id=(gx + dx, gy + dy),
                device_id_type=MESH,
            )
            copies.append(copy)
            pl.when(there(dx, dy))(copy.start)
        return copies

    def wait_halo(v):
        for k, (dx, dy) in enumerate(DIRS):
            @pl.when(there(-dx, -dy))
            def _(k=k, dx=dx, dy=dy):
                halos[v][k].wait_recv()
                if dx and dy:
                    for offset, width, row, columns in corner_strips(-dx, -dy, True, XO, YE):
                        vol[0][v, row, columns] = edge_in[v, k - 4, offset : offset + width]

    loads[0].wait()
    halos = [send_halo(0)]
    loads[1].wait()
    loads[2].wait()

    def make_target(row):
        vol[0][1, XO + row, YE : YE + cols] = lab[row].astype(jnp.float32) * conf[row]

    loop(0, rows, make_target, 8)
    halos.append(send_halo(1))

    def clear_grad(row):
        for i in range(STAGES + 1):
            base[i][row] = jnp.zeros((cols + 24, planes), jnp.float32)
            if 0 < i < STAGES:
                grad[i][row] = jnp.zeros((cols + 24, planes), jnp.float32)

    loop(XO - DEPTH - 1, XO + rows + DEPTH + 1, clear_grad)
    for i in range(STAGES):
        reach = STAGES - i
        for row in (XO - reach - 2, XO - reach - 1, XO + rows + reach, XO + rows + reach + 1):
            for kind in range(7):
                wgt[i, kind, row] = jnp.zeros((cols + 24, planes), jnp.float32)
        for row in (XO - 2, XO - 1, XO + rows, XO + rows + 1):
            hy[i, row] = jnp.zeros((span, planes), jnp.float32)
            for kind in range(3):
                wx[i, kind, row] = jnp.zeros((span, planes), jnp.float32)

    tile = jnp.zeros((8, planes), jnp.float32)

    def clear_sides(row):
        for i in range(STAGES):
            for kind in range(7):
                if i == 0 or kind == YU:
                    wgt[i, kind, row, 0:8] = tile
                if i == 0 or kind == YL:
                    wgt[i, kind, row, cols + 16 : cols + 24] = tile

    loop(XO - STAGES, XO + rows + STAGES, clear_sides)

    def clear_pools(row):
        for i in range(STAGES):
            hz[i, row, YW - 8 : YW] = tile
            hz[i, row, YW + cols : YW + cols + 8] = tile
            for kind in range(3):
                wy[i, kind, row, YW - 8 : YW] = tile
                wy[i, kind, row, YW + cols : YW + cols + 8] = tile

    loop(0, rows, clear_pools)

    def stand_in(i, v):
        reach = DEPTH - i
        every = pl.ds(XO - reach, rows + 2 * reach)

        @pl.when(gy == 0)
        def _():
            vol[i][v, every, YE - 1 : YE] = vol[i][v, every, YE : YE + 1]

        @pl.when(gy == ngy - 1)
        def _():
            vol[i][v, every, YE + cols : YE + cols + 1] = vol[i][v, every, YE + cols - 1 : YE + cols]

        @pl.when(gx == 0)
        def _():
            vol[i][v, XO - 1] = vol[i][v, XO]

        @pl.when(gx == ngx - 1)
        def _():
            vol[i][v, XO + rows] = vol[i][v, XO + rows - 1]

    def before(value, edge):
        return jnp.where(at_first, edge, pltpu.roll(value, 1, 1))

    def after(value):
        return jnp.where(at_last, value, pltpu.roll(value, planes - 1, 1))

    def erode_step(i, v):
        reach = STAGES - i
        done = vol[i + 1]

        def eroded(row):
            mid = vol[i][v, row, 4 : 4 + span]
            least = jnp.minimum(vol[i][v, row - 1, 4 : 4 + span], vol[i][v, row + 1, 4 : 4 + span])
            sides = jnp.minimum(vol[i][v, row, 3 : 3 + span], vol[i][v, row, 5 : 5 + span])
            along = jnp.minimum(before(mid, mid), after(mid))
            return jnp.minimum(jnp.minimum(least, sides), jnp.minimum(along, mid))

        def step(row):
            value = eroded(row)
            if row == XO - 1:
                value = jnp.where(gx == 0, eroded(XO), value)
            if row == XO + rows:
                value = jnp.where(gx == ngx - 1, eroded(XO + rows - 1), value)
            done[v, row, 4 : 4 + span] = value
            for place, inner, found in ((YE - 1, YE, gy == 0), (YE + cols, YE + cols - 1, gy == ngy - 1)):
                done[v, row, place : place + 1] = jnp.where(
                    found, done[v, row, inner : inner + 1], done[v, row, place : place + 1]
                )

        return XO - reach, XO + rows + reach, step

    def delta_step(i, v):
        def step(row):
            most = None
            for x in (-1, 0, 1):
                for y in (-1, 0, 1):
                    value = vol[i + 1][v, XO + row + x, YE + y : YE + y + cols]
                    most = value if most is None else jnp.maximum(most, value)
            most = jnp.maximum(jnp.maximum(before(most, most), most), after(most))
            delta = jnp.maximum(vol[i][v, XO + row, YE : YE + cols] - most, 0.0)
            if i == 0:
                result = delta
            else:
                old = skel[i - 1][v, row]
                result = old + jnp.maximum(delta - old * delta, 0.0)
            skel[i][v, row] = result
            if v == 0:
                dels[i, row] = delta

        return 0, rows, step

    def forward(v):
        wait_halo(v)
        stand_in(0, v)
        straight(erode_step(0, v))
        for i in range(1, STAGES):
            straight(erode_step(i, v), delta_step(i - 1, v))
        straight(delta_step(STAGES - 1, v))

    forward(0)
    def split(total, low, mid, high, first, sign):
        to_high = share(high, first) if sign > 0 else share(first, high)
        to_low = share(low, mid) if sign > 0 else share(mid, low)
        high_part = total * to_high
        rest = total - high_part
        low_part = rest * to_low
        return low_part, high_part, rest - low_part

    def dilate_weights(row):
        for i in range(STAGES):
            low, mid, high = [vol[i + 1][0, XO + row + x, 4 : 4 + span] for x in (-1, 0, 1)]
            first = jnp.maximum(low, mid)
            to_low, to_high, to_mid = split(1.0, low, mid, high, first, -1)
            wx[i, LO, XO + row] = to_low
            wx[i, UP, XO + row] = to_high
            wx[i, MID, XO + row] = to_mid
            pool[i, row] = jnp.maximum(first, high)

    loop(0, rows, dilate_weights, 4)

    def dilate_weights_2(row):
        below = 1.0
        for i in reversed(range(STAGES)):
            low, mid, high = [pool[i, row, 4 + y : 4 + y + cols] for y in (-1, 0, 1)]
            first = jnp.maximum(low, mid)
            to_low, to_high, to_mid = split(1.0, low, mid, high, first, -1)
            wy[i, LO, row, YW : YW + cols] = to_low
            wy[i, UP, row, YW : YW + cols] = to_high
            wy[i, MID, row, YW : YW + cols] = to_mid
            mid = jnp.maximum(first, high)
            low, high = before(mid, -jnp.inf), after(mid)
            first = jnp.maximum(low, mid)
            to_low, to_high, to_mid = split(1.0, low, mid, high, first, -1)
            wz[i, LO, row] = to_low
            wz[i, UP, row] = jnp.where(at_last, 0.0, to_high)
            wz[i, MID, row] = jnp.where(at_last, to_high + to_mid, to_mid)
            delta = dels[i, row]
            if i > 0:
                old = skel[i - 1][0, row]
                passed = jnp.where(delta - old * delta > 0.0, below, 0.0)
                coefs[i, row] = passed - passed * old
                below = below - passed * delta
            else:
                coefs[i, row] = jnp.where(delta > 0.0, below, 0.0)

    loop(0, rows, dilate_weights_2, 4)

    forward(1)

    def add_up(row, sums):
        sum_a, sum_b, sum_c, sum_d = sums
        skel_pred, skel_target = skel[ITERS][0, row], skel[ITERS][1, row]
        return (
            sum_a + skel_pred * vol[0][1, XO + row, YE : YE + cols],
            sum_b + skel_pred,
            sum_c + skel_target * vol[0][0, XO + row, YE : YE + cols],
            sum_d + skel_target,
        )

    sums = (jnp.zeros((cols, planes), jnp.float32),) * 4
    for row in range(rows):
        sums = add_up(row, sums)
    part[...] = jnp.zeros_like(part)
    for k in range(4):
        part[k : k + 1] = jnp.sum(sums[k], axis=0, keepdims=True)

    slots_y[gy] = part[...]
    copies_y = []
    for k in range(1, ngy):
        copy = pltpu.make_async_remote_copy(
            src_ref=part, dst_ref=slots_y.at[gy], send_sem=sy_send.at[k], recv_sem=sy_recv.at[k],
            device_id=(gx, lax.rem(gy + k, ngy)), device_id_type=MESH,
        )
        copy.start()
        copies_y.append(copy)

    def erode_weights(i):
        reach = STAGES - i
        mine = slice(8, 8 + span)

        def step(row):
            mid = vol[i][0, row, 4 : 4 + span]
            x_low, x_high = vol[i][0, row - 1, 4 : 4 + span], vol[i][0, row + 1, 4 : 4 + span]
            y_low, y_high = vol[i][0, row, 3 : 3 + span], vol[i][0, row, 5 : 5 + span]
            z_low, z_high = before(mid, jnp.inf), after(mid)
            x_first, y_first, z_first = [jnp.minimum(low, mid) for low in (x_low, y_low, z_low)]
            x_pool, y_pool = jnp.minimum(x_first, x_high), jnp.minimum(y_first, y_high)
            z_pool = jnp.minimum(z_first, z_high)
            to_z = share(z_pool, jnp.minimum(x_pool, y_pool))
            rest = 1.0 - to_z
            to_y = rest * share(y_pool, x_pool)
            x_parts = split(rest - to_y, x_low, mid, x_high, x_first, 1)
            y_parts = split(to_y, y_low, mid, y_high, y_first, 1)
            z_parts = split(to_z, z_low, mid, z_high, z_first, 1)
            wgt[i, XL, row, mine] = x_parts[0]
            wgt[i, XU, row, mine] = x_parts[1]
            wgt[i, YL, row, mine] = y_parts[0]
            wgt[i, YU, row, mine] = y_parts[1]
            wgt[i, ZL, row, mine] = z_parts[0]
            wgt[i, ZU, row, mine] = jnp.where(at_last, 0.0, z_parts[1])
            centre = x_parts[2] + y_parts[2] + z_parts[2]
            wgt[i, CC, row, mine] = jnp.where(at_last, centre + z_parts[1], centre)

        halves((XO - reach, XO + rows + reach, step))

    def fold():
        mine = slice(8, 8 + span)

        def columns(edge, kind, pool_kind):
            at = pl.ds(edge, 1)
            for i in range(STAGES):
                reach = STAGES - i
                every = pl.ds(XO - reach, rows + 2 * reach)
                wgt[i, CC, every, at] = wgt[i, CC, every, at] + wgt[i, kind, every, at]
                wgt[i, kind, every, at] = jnp.zeros((rows + 2 * reach, 1, planes), jnp.float32)
                wy[i, MID, :, at] = wy[i, MID, :, at] + wy[i, pool_kind, :, at]
                wy[i, pool_kind, :, at] = jnp.zeros((rows, 1, planes), jnp.float32)

        def along_rows(edge, kind, pool_kind):
            for i in range(STAGES):
                wgt[i, CC, edge, mine] = wgt[i, CC, edge, mine] + wgt[i, kind, edge, mine]
                wgt[i, kind, edge, mine] = jnp.zeros((span, planes), jnp.float32)
                wx[i, MID, edge] = wx[i, MID, edge] + wx[i, pool_kind, edge]
                wx[i, pool_kind, edge] = jnp.zeros((span, planes), jnp.float32)

        pl.when(gy == 0)(lambda: columns(YW, YL, LO))
        pl.when(gy == ngy - 1)(lambda: columns(YW + cols - 1, YU, UP))
        pl.when(gx == 0)(lambda: along_rows(XO, XL, LO))
        pl.when(gx == ngx - 1)(lambda: along_rows(XO + rows - 1, XU, UP))

    erode_weights(0)

    for copy in copies_y:
        copy.wait()
    total = slots_y[0]
    for k in range(1, ngy):
        total = total + slots_y[k]
    part[...] = total
    slots_x[gx] = total
    copies_x = []
    for k in range(1, ngx):
        copy = pltpu.make_async_remote_copy(
            src_ref=part, dst_ref=slots_x.at[gx], send_sem=sx_send.at[k], recv_sem=sx_recv.at[k],
            device_id=(lax.rem(gx + k, ngx), gy), device_id_type=MESH,
        )
        copy.start()
        copies_x.append(copy)

    for i in range(1, STAGES):
        erode_weights(i)
    fold()

    for copy in copies_x:
        copy.wait()
    total = slots_x[0]
    for k in range(1, ngx):
        total = total + slots_x[k]
    sum_a, sum_b, sum_c, sum_d = [jnp.sum(total[k : k + 1], axis=1, keepdims=True) for k in range(4)]
    precision = (sum_a + 1.0) / (sum_b + 1.0)
    sensitivity = (sum_c + 1.0) / (sum_d + 1.0)
    together = precision + sensitivity
    loss[...] = 1.0 - 2.0 * precision * sensitivity / together
    cells = float(rows * ngx * cols * ngy * planes)
    coef_pred = cells * (-2.0 * sensitivity * sensitivity / (together * together)) / (sum_b + 1.0)
    coef_target = cells * (-2.0 * precision * precision / (together * together)) / (sum_d + 1.0)
    precision, coef_pred, coef_target = [
        jnp.broadcast_to(value, (cols, planes)) for value in (precision, coef_pred, coef_target)
    ]

    def start_back(row):
        cotangent = coef_pred * (vol[0][1, XO + row, YE : YE + cols] - precision)
        for i in range(STAGES):
            given = cotangent * coefs[i, row]
            base[i][XO + row, YW : YW + cols] = given
            hz[i, row, YW : YW + cols] = -(
                given * wz[i, MID, row]
                + pltpu.roll(given * wz[i, LO, row], planes - 1, 1)
                + pltpu.roll(given * wz[i, UP, row], 1, 1)
            )

    loop(0, rows, start_back, 4)

    def back_columns(row):
        for i in range(STAGES):
            hy[i, XO + row] = (
                wy[i, MID, row, 8 : 8 + span] * hz[i, row, 8 : 8 + span]
                + wy[i, LO, row, 9 : 9 + span] * hz[i, row, 9 : 9 + span]
                + wy[i, UP, row, 7 : 7 + span] * hz[i, row, 7 : 7 + span]
            )

    loop(0, rows, back_columns, 4)

    def back_rows(row):
        for i in range(STAGES):
            base[i + 1][row, 8 : 8 + span] = base[i + 1][row, 8 : 8 + span] + (
                wx[i, MID, row] * hy[i, row]
                + wx[i, LO, row + 1] * hy[i, row + 1]
                + wx[i, UP, row - 1] * hy[i, row - 1]
            )

    straight((XO - 1, XO + rows + 1, back_rows))

    def gather(i, row, low, length):
        source = grad[i + 1] if i + 1 < STAGES else base[i + 1]
        here = slice(low, low + length)
        up, down = slice(low + 1, low + 1 + length), slice(low - 1, low - 1 + length)
        value = source[row, here]
        return (
            base[i][row, here]
            + wgt[i, CC, row, here] * value
            + wgt[i, XL, row + 1, here] * source[row + 1, here]
            + wgt[i, XU, row - 1, here] * source[row - 1, here]
            + wgt[i, YL, row, up] * source[row, up]
            + wgt[i, YU, row, down] * source[row, down]
            + pltpu.roll(wgt[i, ZL, row, here] * value, planes - 1, 1)
            + pltpu.roll(wgt[i, ZU, row, here] * value, 1, 1)
        )

    for i in reversed(range(1, STAGES)):
        def step(row, i=i):
            grad[i][row, 8 : 8 + span] = gather(i, row, 8, span)

        straight((XO - DEPTH + i, XO + rows + DEPTH - i, step))

    def last_step(row):
        final[row] = gather(0, row, YW - 8, cols + 16)

    def send_back(k):
        dx, dy = DIRS[k]
        if dx and dy:
            for offset, width, row, columns in corner_strips(dx, dy, True, XO, YE):
                back_out[k - 4, offset : offset + width] = final[row, columns]
            source, place = back_out.at[k - 4], got_c.at[k - 4]
        else:
            source = final.at[strip(dx, rows, XO, DEPTH, True), strip(dy, cols, YE, 8, True)]
            place = got_x.at[k] if dx else got_y.at[k - 2]
        copy = pltpu.make_async_remote_copy(
            src_ref=source,
            dst_ref=place,
            send_sem=g_send.at[k],
            recv_sem=g_recv.at[k],
            device_id=(gx + dx, gy + dy),
            device_id_type=MESH,
        )
        pl.when(there(dx, dy))(copy.start)
        return copy

    returns = {}
    for side, low in enumerate((XO - DEPTH, XO + rows)):
        for row in range(low, low + DEPTH):
            last_step(row)
        returns[side] = send_back(side)
    for k in range(4, 8):
        returns[k] = send_back(k)

    def middle_step(row):
        value = gather(0, XO + row, YW - 8, cols + 16)
        final[XO + row] = value
        out[row] = value[8 : 8 + cols] + coef_target * skel[ITERS][1, row]

    halves((0, rows, middle_step))
    for k in (2, 3):
        returns[k] = send_back(k)

    for k, (dx, dy) in enumerate(DIRS):
        @pl.when(there(-dx, -dy))
        def _(k=k, dx=dx, dy=dy):
            returns[k].wait_recv()
            if dx and dy:
                for offset, width, row, columns in corner_strips(-dx, -dy, False, 0, 0):
                    out[row, columns] = out[row, columns] + got_c[k - 4, offset : offset + width]
            else:
                at = (strip(-dx, rows, 0, DEPTH, False), strip(-dy, cols, 0, 8, False))
                out[at] = out[at] + (got_x[k] if dx else got_y[k - 2])

    for k, (dx, dy) in enumerate(DIRS):
        @pl.when(there(dx, dy))
        def _(k=k):
            halos[0][k].wait_send()
            halos[1][k].wait_send()
            returns[k].wait_send()


def body(prediction, label_mask, confidence):
    rows, cols, planes = prediction.shape
    ngx, ngy = lax.axis_size("gx"), lax.axis_size("gy")
    f32 = jnp.float32
    wide = rows + 2 * XO
    corner = (DEPTH * (DEPTH + 1) // 2 + 7) // 8 * 8
    dma = pltpu.SemaphoreType.DMA
    gradient, loss = pl.pallas_call(
        functools.partial(kernel, (rows, cols, planes, ngx, ngy)),
        out_shape=(jax.ShapeDtypeStruct((rows, cols, planes), f32), jax.ShapeDtypeStruct((1, 1), f32)),
        in_specs=[pl.BlockSpec(memory_space=pl.ANY)] * 3,
        out_specs=(pl.BlockSpec(memory_space=pltpu.VMEM), pl.BlockSpec(memory_space=pltpu.VMEM)),
        scratch_shapes=[
            [pltpu.VMEM((2, wide, cols + 16, planes), f32)] * (STAGES + 1),
            pltpu.VMEM((rows, cols, planes), jnp.int32),
            pltpu.VMEM((rows, cols, planes), f32),
            [pltpu.VMEM((2, rows, cols, planes), f32)] * STAGES,
            pltpu.VMEM((STAGES, rows, cols, planes), f32),
            pltpu.VMEM((STAGES, rows, cols, planes), f32),
            pltpu.VMEM((STAGES, rows, cols + 8, planes), f32),
            pltpu.VMEM((STAGES, 7, wide, cols + 24, planes), f32),
            pltpu.VMEM((STAGES, 3, wide, cols + 8, planes), f32),
            pltpu.VMEM((STAGES, 3, rows, cols + 24, planes), f32),
            pltpu.VMEM((STAGES, 3, rows, cols, planes), f32),
            [pltpu.VMEM((wide, cols + 24, planes), f32)] * (STAGES + 1),
            [pltpu.VMEM((wide, cols + 24, planes), f32)] * STAGES,
            pltpu.VMEM((STAGES, rows, cols + 24, planes), f32),
            pltpu.VMEM((STAGES, wide, cols + 8, planes), f32),
            pltpu.VMEM((wide, cols + 16, planes), f32),
            pltpu.VMEM((8, planes), f32),
            pltpu.VMEM((ngy, 8, planes), f32),
            pltpu.VMEM((ngx, 8, planes), f32),
            pltpu.VMEM((2, DEPTH, cols, planes), f32),
            pltpu.VMEM((2, rows, 8, planes), f32),
            pltpu.VMEM((4, corner, planes), f32),
            pltpu.VMEM((2, 4, corner, planes), f32),
            pltpu.VMEM((2, 4, corner, planes), f32),
            pltpu.VMEM((4, corner, planes), f32),
            dma((3,)),
            dma((16,)),
            dma((16,)),
            dma((ngy,)),
            dma((ngy,)),
            dma((ngx,)),
            dma((ngx,)),
            dma((8,)),
            dma((8,)),
        ],
        compiler_params=pltpu.CompilerParams(
            collective_id=0, has_side_effects=True, vmem_limit_bytes=60 * 1024 * 1024
        ),
    )(prediction, label_mask, confidence)
    return gradient, loss[0, 0]


def solution(mesh):
    placed = (P("gx", "gy", None), P("gx", "gy", None), P("gx", "gy", None))
    return jax.shard_map(
        body, mesh=mesh, in_specs=placed, out_specs=(P("gx", "gy", None), P()), check_vma=False
    )
```

```python
import functools

import jax
import jax.numpy as jnp
from jax import lax
from jax.experimental import pallas as pl
from jax.experimental.pallas import tpu as pltpu
from jax.sharding import PartitionSpec as P

ITERS = 3
STAGES = ITERS + 1
DEPTH = ITERS + 2
XO = 8
YE = 8
YW = 12
MESH = pl.DeviceIdType.MESH
XL, XU, YL, YU, ZL, ZU, CC = range(7)
LO, UP, MID = range(3)
DIRS = ((-1, 0), (1, 0), (0, -1), (0, 1), (-1, -1), (-1, 1), (1, -1), (1, 1))


def share(winner, other):
    return jnp.where(winner < other, 1.0, jnp.where(winner == other, 0.5, 0.0))


def loop(low, high, body, step=4):
    count = (high - low) // step

    if count == 1:
        for row in range(low, low + step):
            body(row)
    else:

        @pl.loop(0, count)
        def _(index):
            for k in range(step):
                body(low + index * step + k)

    for row in range(low + count * step, high):
        body(row)


def halves(*parts):
    @pl.loop(0, 2)
    def _(index):
        for low, high, body in parts:
            step = (high - low) // 2
            for k in range(step):
                body(low + index * step + k)

    for low, high, body in parts:
        if (high - low) % 2:
            body(high - 1)


def straight(*parts):
    for low, high, body in parts:
        for row in range(low, high):
            body(row)


def kernel(
    sizes, pred_hbm, label_hbm, conf_hbm, out, loss,
    vol, lab, conf, skel, dels, coefs, pool, wgt, wx, wy, wz, base, grad, hz, hy, final,
    part, slots_y, slots_x, got_x, got_y, got_c, edge_out, edge_in, back_out,
    in_sem, halo_send, halo_recv, sy_send, sy_recv, sx_send, sx_recv, g_send, g_recv,
):
    rows, cols, planes, ngx, ngy = sizes
    gx, gy = lax.axis_index("gx"), lax.axis_index("gy")
    own_x, own_y, own_w = pl.ds(XO, rows), pl.ds(YE, cols), pl.ds(YW, cols)
    span = cols + 8
    lanes = lax.broadcasted_iota(jnp.int32, (1, planes), 1)
    at_first, at_last = lanes == 0, lanes == planes - 1

    loads = [
        pltpu.make_async_copy(pred_hbm, vol[0].at[0, own_x, own_y], in_sem.at[0]),
        pltpu.make_async_copy(label_hbm, lab, in_sem.at[1]),
        pltpu.make_async_copy(conf_hbm, conf, in_sem.at[2]),
    ]
    for copy in loads:
        copy.start()

    def there(dx, dy):
        found = None
        for d, me, size in ((dx, gx, ngx), (dy, gy, ngy)):
            if d:
                inside = (me > 0) if d < 0 else (me < size - 1)
                found = inside if found is None else jnp.logical_and(found, inside)
        return found

    barrier = pltpu.get_barrier_semaphore()
    for k in range(1, ngx):
        pl.semaphore_signal(barrier, inc=1, device_id=(lax.rem(gx + k, ngx), gy), device_id_type=MESH)
    for k in range(1, ngy):
        pl.semaphore_signal(barrier, inc=1, device_id=(gx, lax.rem(gy + k, ngy)), device_id_type=MESH)
    for dx, dy in DIRS[4:]:
        @pl.when(there(dx, dy))
        def _(dx=dx, dy=dy):
            pl.semaphore_signal(barrier, inc=1, device_id=(gx + dx, gy + dy), device_id_type=MESH)

    corners = 1
    for me, size in ((gx, ngx), (gy, ngy)):
        corners *= lax.div(me + size - 1, size) + lax.div(2 * size - 2 - me, size)
    pl.semaphore_wait(barrier, ngx - 1 + ngy - 1 + corners)

    def strip(d, length, offset, width, outside):
        if d == 0:
            return pl.ds(offset, length)
        if d < 0:
            return pl.ds(offset - width if outside else offset, width)
        return pl.ds(offset + length if outside else offset + length - width, width)

    def corner_strips(dx, dy, outside, x_at, y_at):
        offset, found = 0, []
        for i in range(1, DEPTH + 1):
            width = DEPTH + 1 - i
            if outside:
                row = x_at - i if dx < 0 else x_at + rows + i - 1
                column = y_at - width if dy < 0 else y_at + cols
            else:
                row = x_at + i - 1 if dx < 0 else x_at + rows - i
                column = y_at if dy < 0 else y_at + cols - width
            found.append((offset, width, row, slice(column, column + width)))
            offset += width
        return found

    def send_halo(v):
        copies = []
        for k, (dx, dy) in enumerate(DIRS):
            if dx and dy:
                for offset, width, row, columns in corner_strips(dx, dy, False, XO, YE):
                    edge_out[v, k - 4, offset : offset + width] = vol[0][v, row, columns]
                source, target = edge_out.at[v, k - 4], edge_in.at[v, k - 4]
            else:
                source = vol[0].at[v, strip(dx, rows, XO, DEPTH, False), strip(dy, cols, YE, 8, False)]
                target = vol[0].at[v, strip(-dx, rows, XO, DEPTH, True), strip(-dy, cols, YE, 8, True)]
            copy = pltpu.make_async_remote_copy(
                src_ref=source,
                dst_ref=target,
                send_sem=halo_send.at[8 * v + k],
                recv_sem=halo_recv.at[8 * v + k],
                device_id=(gx + dx, gy + dy),
                device_id_type=MESH,
            )
            copies.append(copy)
            pl.when(there(dx, dy))(copy.start)
        return copies

    def wait_halo(v):
        for k, (dx, dy) in enumerate(DIRS):
            @pl.when(there(-dx, -dy))
            def _(k=k, dx=dx, dy=dy):
                halos[v][k].wait_recv()
                if dx and dy:
                    for offset, width, row, columns in corner_strips(-dx, -dy, True, XO, YE):
                        vol[0][v, row, columns] = edge_in[v, k - 4, offset : offset + width]

    loads[0].wait()
    halos = [send_halo(0)]
    loads[1].wait()
    loads[2].wait()

    def make_target(row):
        vol[0][1, XO + row, YE : YE + cols] = lab[row].astype(jnp.float32) * conf[row]

    loop(0, rows, make_target, 8)
    halos.append(send_halo(1))

    def clear_grad(row):
        for i in range(STAGES + 1):
            base[i][row] = jnp.zeros((cols + 24, planes), jnp.float32)
            if 0 < i < STAGES:
                grad[i][row] = jnp.zeros((cols + 24, planes), jnp.float32)

    loop(XO - DEPTH - 1, XO + rows + DEPTH + 1, clear_grad)
    for i in range(STAGES):
        reach = STAGES - i
        for row in (XO - reach - 2, XO - reach - 1, XO + rows + reach, XO + rows + reach + 1):
            for kind in range(7):
                wgt[i, kind, row] = jnp.zeros((cols + 24, planes), jnp.float32)
        for row in (XO - 2, XO - 1, XO + rows, XO + rows + 1):
            hy[i, row] = jnp.zeros((span, planes), jnp.float32)
            for kind in range(3):
                wx[i, kind, row] = jnp.zeros((span, planes), jnp.float32)

    tile = jnp.zeros((8, planes), jnp.float32)

    def clear_sides(row):
        for i in range(STAGES):
            for kind in range(7):
                if i == 0 or kind == YU:
                    wgt[i, kind, row, 0:8] = tile
                if i == 0 or kind == YL:
                    wgt[i, kind, row, cols + 16 : cols + 24] = tile

    loop(XO - STAGES, XO + rows + STAGES, clear_sides)

    def clear_pools(row):
        for i in range(STAGES):
            hz[i, row, YW - 8 : YW] = tile
            hz[i, row, YW + cols : YW + cols + 8] = tile
            for kind in range(3):
                wy[i, kind, row, YW - 8 : YW] = tile
                wy[i, kind, row, YW + cols : YW + cols + 8] = tile

    loop(0, rows, clear_pools)

    def stand_in(i, v):
        reach = DEPTH - i
        every = pl.ds(XO - reach, rows + 2 * reach)

        @pl.when(gy == 0)
        def _():
            vol[i][v, every, YE - 1 : YE] = vol[i][v, every, YE : YE + 1]

        @pl.when(gy == ngy - 1)
        def _():
            vol[i][v, every, YE + cols : YE + cols + 1] = vol[i][v, every, YE + cols - 1 : YE + cols]

        @pl.when(gx == 0)
        def _():
            vol[i][v, XO - 1] = vol[i][v, XO]

        @pl.when(gx == ngx - 1)
        def _():
            vol[i][v, XO + rows] = vol[i][v, XO + rows - 1]

    def before(value, edge):
        return jnp.where(at_first, edge, pltpu.roll(value, 1, 1))

    def after(value):
        return jnp.where(at_last, value, pltpu.roll(value, planes - 1, 1))

    def erode_step(i, v):
        reach = STAGES - i
        done = vol[i + 1]

        def eroded(row):
            mid = vol[i][v, row, 4 : 4 + span]
            least = jnp.minimum(vol[i][v, row - 1, 4 : 4 + span], vol[i][v, row + 1, 4 : 4 + span])
            sides = jnp.minimum(vol[i][v, row, 3 : 3 + span], vol[i][v, row, 5 : 5 + span])
            along = jnp.minimum(before(mid, mid), after(mid))
            return jnp.minimum(jnp.minimum(least, sides), jnp.minimum(along, mid))

        def step(row):
            value = eroded(row)
            if row == XO - 1:
                value = jnp.where(gx == 0, eroded(XO), value)
            if row == XO + rows:
                value = jnp.where(gx == ngx - 1, eroded(XO + rows - 1), value)
            done[v, row, 4 : 4 + span] = value
            for place, inner, found in ((YE - 1, YE, gy == 0), (YE + cols, YE + cols - 1, gy == ngy - 1)):
                done[v, row, place : place + 1] = jnp.where(
                    found, done[v, row, inner : inner + 1], done[v, row, place : place + 1]
                )

        return XO - reach, XO + rows + reach, step

    def delta_step(i, v):
        def step(row):
            most = None
            for x in (-1, 0, 1):
                for y in (-1, 0, 1):
                    value = vol[i + 1][v, XO + row + x, YE + y : YE + y + cols]
                    most = value if most is None else jnp.maximum(most, value)
            most = jnp.maximum(jnp.maximum(before(most, most), most), after(most))
            delta = jnp.maximum(vol[i][v, XO + row, YE : YE + cols] - most, 0.0)
            if i == 0:
                result = delta
            else:
                old = skel[i - 1][v, row]
                result = old + jnp.maximum(delta - old * delta, 0.0)
            skel[i][v, row] = result
            if v == 0:
                dels[i, row] = delta

        return 0, rows, step

    def forward(v):
        wait_halo(v)
        stand_in(0, v)
        straight(erode_step(0, v))
        for i in range(1, STAGES):
            straight(erode_step(i, v), delta_step(i - 1, v))
        straight(delta_step(STAGES - 1, v))

    forward(0)
    forward(1)

    def add_up(row, sums):
        sum_a, sum_b, sum_c, sum_d = sums
        skel_pred, skel_target = skel[ITERS][0, row], skel[ITERS][1, row]
        return (
            sum_a + skel_pred * vol[0][1, XO + row, YE : YE + cols],
            sum_b + skel_pred,
            sum_c + skel_target * vol[0][0, XO + row, YE : YE + cols],
            sum_d + skel_target,
        )

    sums = (jnp.zeros((cols, planes), jnp.float32),) * 4
    for row in range(rows):
        sums = add_up(row, sums)
    part[...] = jnp.zeros_like(part)
    for k in range(4):
        part[k : k + 1] = jnp.sum(sums[k], axis=0, keepdims=True)

    slots_y[gy] = part[...]
    copies_y = []
    for k in range(1, ngy):
        copy = pltpu.make_async_remote_copy(
            src_ref=part, dst_ref=slots_y.at[gy], send_sem=sy_send.at[k], recv_sem=sy_recv.at[k],
            device_id=(gx, lax.rem(gy + k, ngy)), device_id_type=MESH,
        )
        copy.start()
        copies_y.append(copy)

    def split(total, low, mid, high, first, sign):
        to_high = share(high, first) if sign > 0 else share(first, high)
        to_low = share(low, mid) if sign > 0 else share(mid, low)
        high_part = total * to_high
        rest = total - high_part
        low_part = rest * to_low
        return low_part, high_part, rest - low_part

    def dilate_weights(row):
        for i in range(STAGES):
            low, mid, high = [vol[i + 1][0, XO + row + x, 4 : 4 + span] for x in (-1, 0, 1)]
            first = jnp.maximum(low, mid)
            to_low, to_high, to_mid = split(1.0, low, mid, high, first, -1)
            wx[i, LO, XO + row] = to_low
            wx[i, UP, XO + row] = to_high
            wx[i, MID, XO + row] = to_mid
            pool[i, row] = jnp.maximum(first, high)

    loop(0, rows, dilate_weights, 4)

    def dilate_weights_2(row):
        below = 1.0
        for i in reversed(range(STAGES)):
            low, mid, high = [pool[i, row, 4 + y : 4 + y + cols] for y in (-1, 0, 1)]
            first = jnp.maximum(low, mid)
            to_low, to_high, to_mid = split(1.0, low, mid, high, first, -1)
            wy[i, LO, row, YW : YW + cols] = to_low
            wy[i, UP, row, YW : YW + cols] = to_high
            wy[i, MID, row, YW : YW + cols] = to_mid
            mid = jnp.maximum(first, high)
            low, high = before(mid, -jnp.inf), after(mid)
            first = jnp.maximum(low, mid)
            to_low, to_high, to_mid = split(1.0, low, mid, high, first, -1)
            wz[i, LO, row] = to_low
            wz[i, UP, row] = jnp.where(at_last, 0.0, to_high)
            wz[i, MID, row] = jnp.where(at_last, to_high + to_mid, to_mid)
            delta = dels[i, row]
            if i > 0:
                old = skel[i - 1][0, row]
                passed = jnp.where(delta - old * delta > 0.0, below, 0.0)
                coefs[i, row] = passed - passed * old
                below = below - passed * delta
            else:
                coefs[i, row] = jnp.where(delta > 0.0, below, 0.0)

    loop(0, rows, dilate_weights_2, 4)

    def erode_weights(i):
        reach = STAGES - i
        mine = slice(8, 8 + span)

        def step(row):
            mid = vol[i][0, row, 4 : 4 + span]
            x_low, x_high = vol[i][0, row - 1, 4 : 4 + span], vol[i][0, row + 1, 4 : 4 + span]
            y_low, y_high = vol[i][0, row, 3 : 3 + span], vol[i][0, row, 5 : 5 + span]
            z_low, z_high = before(mid, jnp.inf), after(mid)
            x_first, y_first, z_first = [jnp.minimum(low, mid) for low in (x_low, y_low, z_low)]
            x_pool, y_pool = jnp.minimum(x_first, x_high), jnp.minimum(y_first, y_high)
            z_pool = jnp.minimum(z_first, z_high)
            to_z = share(z_pool, jnp.minimum(x_pool, y_pool))
            rest = 1.0 - to_z
            to_y = rest * share(y_pool, x_pool)
            x_parts = split(rest - to_y, x_low, mid, x_high, x_first, 1)
            y_parts = split(to_y, y_low, mid, y_high, y_first, 1)
            z_parts = split(to_z, z_low, mid, z_high, z_first, 1)
            wgt[i, XL, row, mine] = x_parts[0]
            wgt[i, XU, row, mine] = x_parts[1]
            wgt[i, YL, row, mine] = y_parts[0]
            wgt[i, YU, row, mine] = y_parts[1]
            wgt[i, ZL, row, mine] = z_parts[0]
            wgt[i, ZU, row, mine] = jnp.where(at_last, 0.0, z_parts[1])
            centre = x_parts[2] + y_parts[2] + z_parts[2]
            wgt[i, CC, row, mine] = jnp.where(at_last, centre + z_parts[1], centre)

        halves((XO - reach, XO + rows + reach, step))

    def fold():
        mine = slice(8, 8 + span)

        def columns(edge, kind, pool_kind):
            at = pl.ds(edge, 1)
            for i in range(STAGES):
                reach = STAGES - i
                every = pl.ds(XO - reach, rows + 2 * reach)
                wgt[i, CC, every, at] = wgt[i, CC, every, at] + wgt[i, kind, every, at]
                wgt[i, kind, every, at] = jnp.zeros((rows + 2 * reach, 1, planes), jnp.float32)
                wy[i, MID, :, at] = wy[i, MID, :, at] + wy[i, pool_kind, :, at]
                wy[i, pool_kind, :, at] = jnp.zeros((rows, 1, planes), jnp.float32)

        def along_rows(edge, kind, pool_kind):
            for i in range(STAGES):
                wgt[i, CC, edge, mine] = wgt[i, CC, edge, mine] + wgt[i, kind, edge, mine]
                wgt[i, kind, edge, mine] = jnp.zeros((span, planes), jnp.float32)
                wx[i, MID, edge] = wx[i, MID, edge] + wx[i, pool_kind, edge]
                wx[i, pool_kind, edge] = jnp.zeros((span, planes), jnp.float32)

        pl.when(gy == 0)(lambda: columns(YW, YL, LO))
        pl.when(gy == ngy - 1)(lambda: columns(YW + cols - 1, YU, UP))
        pl.when(gx == 0)(lambda: along_rows(XO, XL, LO))
        pl.when(gx == ngx - 1)(lambda: along_rows(XO + rows - 1, XU, UP))

    erode_weights(0)

    for copy in copies_y:
        copy.wait()
    total = slots_y[0]
    for k in range(1, ngy):
        total = total + slots_y[k]
    part[...] = total
    slots_x[gx] = total
    copies_x = []
    for k in range(1, ngx):
        copy = pltpu.make_async_remote_copy(
            src_ref=part, dst_ref=slots_x.at[gx], send_sem=sx_send.at[k], recv_sem=sx_recv.at[k],
            device_id=(lax.rem(gx + k, ngx), gy), device_id_type=MESH,
        )
        copy.start()
        copies_x.append(copy)

    for i in range(1, STAGES):
        erode_weights(i)
    fold()

    for copy in copies_x:
        copy.wait()
    total = slots_x[0]
    for k in range(1, ngx):
        total = total + slots_x[k]
    sum_a, sum_b, sum_c, sum_d = [jnp.sum(total[k : k + 1], axis=1, keepdims=True) for k in range(4)]
    precision = (sum_a + 1.0) / (sum_b + 1.0)
    sensitivity = (sum_c + 1.0) / (sum_d + 1.0)
    together = precision + sensitivity
    loss[...] = 1.0 - 2.0 * precision * sensitivity / together
    cells = float(rows * ngx * cols * ngy * planes)
    coef_pred = cells * (-2.0 * sensitivity * sensitivity / (together * together)) / (sum_b + 1.0)
    coef_target = cells * (-2.0 * precision * precision / (together * together)) / (sum_d + 1.0)
    precision, coef_pred, coef_target = [
        jnp.broadcast_to(value, (cols, planes)) for value in (precision, coef_pred, coef_target)
    ]

    def start_back(row):
        cotangent = coef_pred * (vol[0][1, XO + row, YE : YE + cols] - precision)
        for i in range(STAGES):
            given = cotangent * coefs[i, row]
            base[i][XO + row, YW : YW + cols] = given
            hz[i, row, YW : YW + cols] = -(
                given * wz[i, MID, row]
                + pltpu.roll(given * wz[i, LO, row], planes - 1, 1)
                + pltpu.roll(given * wz[i, UP, row], 1, 1)
            )

    loop(0, rows, start_back, 4)

    def back_columns(row):
        for i in range(STAGES):
            hy[i, XO + row] = (
                wy[i, MID, row, 8 : 8 + span] * hz[i, row, 8 : 8 + span]
                + wy[i, LO, row, 9 : 9 + span] * hz[i, row, 9 : 9 + span]
                + wy[i, UP, row, 7 : 7 + span] * hz[i, row, 7 : 7 + span]
            )

    loop(0, rows, back_columns, 4)

    def back_rows(row):
        for i in range(STAGES):
            base[i + 1][row, 8 : 8 + span] = base[i + 1][row, 8 : 8 + span] + (
                wx[i, MID, row] * hy[i, row]
                + wx[i, LO, row + 1] * hy[i, row + 1]
                + wx[i, UP, row - 1] * hy[i, row - 1]
            )

    straight((XO - 1, XO + rows + 1, back_rows))

    def gather(i, row, low, length):
        source = grad[i + 1] if i + 1 < STAGES else base[i + 1]
        here = slice(low, low + length)
        up, down = slice(low + 1, low + 1 + length), slice(low - 1, low - 1 + length)
        value = source[row, here]
        return (
            base[i][row, here]
            + wgt[i, CC, row, here] * value
            + wgt[i, XL, row + 1, here] * source[row + 1, here]
            + wgt[i, XU, row - 1, here] * source[row - 1, here]
            + wgt[i, YL, row, up] * source[row, up]
            + wgt[i, YU, row, down] * source[row, down]
            + pltpu.roll(wgt[i, ZL, row, here] * value, planes - 1, 1)
            + pltpu.roll(wgt[i, ZU, row, here] * value, 1, 1)
        )

    for i in reversed(range(1, STAGES)):
        def step(row, i=i):
            grad[i][row, 8 : 8 + span] = gather(i, row, 8, span)

        straight((XO - DEPTH + i, XO + rows + DEPTH - i, step))

    def last_step(row):
        final[row] = gather(0, row, YW - 8, cols + 16)

    def send_back(k):
        dx, dy = DIRS[k]
        if dx and dy:
            for offset, width, row, columns in corner_strips(dx, dy, True, XO, YE):
                back_out[k - 4, offset : offset + width] = final[row, columns]
            source, place = back_out.at[k - 4], got_c.at[k - 4]
        else:
            source = final.at[strip(dx, rows, XO, DEPTH, True), strip(dy, cols, YE, 8, True)]
            place = got_x.at[k] if dx else got_y.at[k - 2]
        copy = pltpu.make_async_remote_copy(
            src_ref=source,
            dst_ref=place,
            send_sem=g_send.at[k],
            recv_sem=g_recv.at[k],
            device_id=(gx + dx, gy + dy),
            device_id_type=MESH,
        )
        pl.when(there(dx, dy))(copy.start)
        return copy

    returns = {}
    for side, low in enumerate((XO - DEPTH, XO + rows)):
        for row in range(low, low + DEPTH):
            last_step(row)
        returns[side] = send_back(side)
    for k in range(4, 8):
        returns[k] = send_back(k)

    def middle_step(row):
        value = gather(0, XO + row, YW - 8, cols + 16)
        final[XO + row] = value
        out[row] = value[8 : 8 + cols] + coef_target * skel[ITERS][1, row]

    halves((0, rows, middle_step))
    for k in (2, 3):
        returns[k] = send_back(k)

    for k, (dx, dy) in enumerate(DIRS):
        @pl.when(there(-dx, -dy))
        def _(k=k, dx=dx, dy=dy):
            returns[k].wait_recv()
            if dx and dy:
                for offset, width, row, columns in corner_strips(-dx, -dy, False, 0, 0):
                    out[row, columns] = out[row, columns] + got_c[k - 4, offset : offset + width]
            else:
                at = (strip(-dx, rows, 0, DEPTH, False), strip(-dy, cols, 0, 8, False))
                out[at] = out[at] + (got_x[k] if dx else got_y[k - 2])

    for k, (dx, dy) in enumerate(DIRS):
        @pl.when(there(dx, dy))
        def _(k=k):
            halos[0][k].wait_send()
            halos[1][k].wait_send()
            returns[k].wait_send()


def body(prediction, label_mask, confidence):
    rows, cols, planes = prediction.shape
    ngx, ngy = lax.axis_size("gx"), lax.axis_size("gy")
    f32 = jnp.float32
    wide = rows + 2 * XO
    corner = (DEPTH * (DEPTH + 1) // 2 + 7) // 8 * 8
    dma = pltpu.SemaphoreType.DMA
    gradient, loss = pl.pallas_call(
        functools.partial(kernel, (rows, cols, planes, ngx, ngy)),
        out_shape=(jax.ShapeDtypeStruct((rows, cols, planes), f32), jax.ShapeDtypeStruct((1, 1), f32)),
        in_specs=[pl.BlockSpec(memory_space=pltpu.HBM)] * 3,
        out_specs=(pl.BlockSpec(memory_space=pltpu.VMEM), pl.BlockSpec(memory_space=pltpu.VMEM)),
        scratch_shapes=[
            [pltpu.VMEM((2, wide, cols + 16, planes), f32)] * (STAGES + 1),
            pltpu.VMEM((rows, cols, planes), jnp.int32),
            pltpu.VMEM((rows, cols, planes), f32),
            [pltpu.VMEM((2, rows, cols, planes), f32)] * STAGES,
            pltpu.VMEM((STAGES, rows, cols, planes), f32),
            pltpu.VMEM((STAGES, rows, cols, planes), f32),
            pltpu.VMEM((STAGES, rows, cols + 8, planes), f32),
            pltpu.VMEM((STAGES, 7, wide, cols + 24, planes), f32),
            pltpu.VMEM((STAGES, 3, wide, cols + 8, planes), f32),
            pltpu.VMEM((STAGES, 3, rows, cols + 24, planes), f32),
            pltpu.VMEM((STAGES, 3, rows, cols, planes), f32),
            [pltpu.VMEM((wide, cols + 24, planes), f32)] * (STAGES + 1),
            [pltpu.VMEM((wide, cols + 24, planes), f32)] * STAGES,
            pltpu.VMEM((STAGES, rows, cols + 24, planes), f32),
            pltpu.VMEM((STAGES, wide, cols + 8, planes), f32),
            pltpu.VMEM((wide, cols + 16, planes), f32),
            pltpu.VMEM((8, planes), f32),
            pltpu.VMEM((ngy, 8, planes), f32),
            pltpu.VMEM((ngx, 8, planes), f32),
            pltpu.VMEM((2, DEPTH, cols, planes), f32),
            pltpu.VMEM((2, rows, 8, planes), f32),
            pltpu.VMEM((4, corner, planes), f32),
            pltpu.VMEM((2, 4, corner, planes), f32),
            pltpu.VMEM((2, 4, corner, planes), f32),
            pltpu.VMEM((4, corner, planes), f32),
            dma((3,)),
            dma((16,)),
            dma((16,)),
            dma((ngy,)),
            dma((ngy,)),
            dma((ngx,)),
            dma((ngx,)),
            dma((8,)),
            dma((8,)),
        ],
        compiler_params=pltpu.CompilerParams(
            collective_id=0, has_side_effects=True, vmem_limit_bytes=50 * 1024 * 1024
        ),
    )(*(pltpu.with_memory_space_constraint(value, pltpu.HBM) for value in (prediction, label_mask, confidence)))
    return gradient, loss[0, 0]


def solution(mesh):
    placed = (P("gx", "gy", None), P("gx", "gy", None), P("gx", "gy", None))
    return jax.shard_map(
        body, mesh=mesh, in_specs=placed, out_specs=(P("gx", "gy", None), P()), check_vma=False
    )
```

```python
import functools

import jax
import jax.numpy as jnp
from jax import lax
from jax.experimental import pallas as pl
from jax.experimental.pallas import tpu as pltpu
from jax.sharding import PartitionSpec as P

ITERS = 3
STAGES = ITERS + 1
DEPTH = ITERS + 2
XO = 8
YE = 8
YW = 12
MESH = pl.DeviceIdType.MESH
XL, XU, YL, YU, ZL, ZU, CC = range(7)
LO, UP, MID = range(3)
DIRS = ((-1, 0), (1, 0), (0, -1), (0, 1), (-1, -1), (-1, 1), (1, -1), (1, 1))


def share(winner, other):
    return jnp.where(winner < other, 1.0, jnp.where(winner == other, 0.5, 0.0))


def loop(low, high, body, step=4):
    count = (high - low) // step

    if count == 1:
        for row in range(low, low + step):
            body(row)
    else:

        @pl.loop(0, count)
        def _(index):
            for k in range(step):
                body(low + index * step + k)

    for row in range(low + count * step, high):
        body(row)


def halves(*parts):
    @pl.loop(0, 2)
    def _(index):
        for low, high, body in parts:
            step = (high - low) // 2
            for k in range(step):
                body(low + index * step + k)

    for low, high, body in parts:
        if (high - low) % 2:
            body(high - 1)


def straight(*parts):
    for low, high, body in parts:
        for row in range(low, high):
            body(row)


def kernel(
    sizes, pred_hbm, label_hbm, conf_hbm, out, loss,
    vol, lab, conf, skel, dels, coefs, pool, wgt, wx, wy, wz, base, grad, hz, hy, final,
    part, slots_y, slots_x, got_x, got_y, got_c, edge_out, edge_in, back_out,
    in_sem, halo_send, halo_recv, sy_send, sy_recv, sx_send, sx_recv, g_send, g_recv,
):
    rows, cols, planes, ngx, ngy = sizes
    gx, gy = lax.axis_index("gx"), lax.axis_index("gy")
    own_x, own_y, own_w = pl.ds(XO, rows), pl.ds(YE, cols), pl.ds(YW, cols)
    span = cols + 8
    lanes = lax.broadcasted_iota(jnp.int32, (1, planes), 1)
    at_first, at_last = lanes == 0, lanes == planes - 1

    loads = [
        pltpu.make_async_copy(pred_hbm, vol[0].at[0, own_x, own_y], in_sem.at[0]),
        pltpu.make_async_copy(label_hbm, lab, in_sem.at[1]),
        pltpu.make_async_copy(conf_hbm, conf, in_sem.at[2]),
    ]
    for copy in loads:
        copy.start()

    def there(dx, dy):
        found = None
        for d, me, size in ((dx, gx, ngx), (dy, gy, ngy)):
            if d:
                inside = (me > 0) if d < 0 else (me < size - 1)
                found = inside if found is None else jnp.logical_and(found, inside)
        return found

    barrier = pltpu.get_barrier_semaphore()
    for k in range(1, ngx):
        pl.semaphore_signal(barrier, inc=1, device_id=(lax.rem(gx + k, ngx), gy), device_id_type=MESH)
    for k in range(1, ngy):
        pl.semaphore_signal(barrier, inc=1, device_id=(gx, lax.rem(gy + k, ngy)), device_id_type=MESH)
    for dx, dy in DIRS[4:]:
        @pl.when(there(dx, dy))
        def _(dx=dx, dy=dy):
            pl.semaphore_signal(barrier, inc=1, device_id=(gx + dx, gy + dy), device_id_type=MESH)

    corners = 1
    for me, size in ((gx, ngx), (gy, ngy)):
        corners *= lax.div(me + size - 1, size) + lax.div(2 * size - 2 - me, size)
    pl.semaphore_wait(barrier, ngx - 1 + ngy - 1 + corners)

    def strip(d, length, offset, width, outside):
        if d == 0:
            return pl.ds(offset, length)
        if d < 0:
            return pl.ds(offset - width if outside else offset, width)
        return pl.ds(offset + length if outside else offset + length - width, width)

    def corner_strips(dx, dy, outside, x_at, y_at):
        offset, found = 0, []
        for i in range(1, DEPTH + 1):
            width = DEPTH + 1 - i
            if outside:
                row = x_at - i if dx < 0 else x_at + rows + i - 1
                column = y_at - width if dy < 0 else y_at + cols
            else:
                row = x_at + i - 1 if dx < 0 else x_at + rows - i
                column = y_at if dy < 0 else y_at + cols - width
            found.append((offset, width, row, slice(column, column + width)))
            offset += width
        return found

    def send_halo(v):
        copies = []
        for k, (dx, dy) in enumerate(DIRS):
            if dx and dy:
                for offset, width, row, columns in corner_strips(dx, dy, False, XO, YE):
                    edge_out[v, k - 4, offset : offset + width] = vol[0][v, row, columns]
                source, target = edge_out.at[v, k - 4], edge_in.at[v, k - 4]
            else:
                source = vol[0].at[v, strip(dx, rows, XO, DEPTH, False), strip(dy, cols, YE, 8, False)]
                target = vol[0].at[v, strip(-dx, rows, XO, DEPTH, True), strip(-dy, cols, YE, 8, True)]
            copy = pltpu.make_async_remote_copy(
                src_ref=source,
                dst_ref=target,
                send_sem=halo_send.at[8 * v + k],
                recv_sem=halo_recv.at[8 * v + k],
                device_id=(gx + dx, gy + dy),
                device_id_type=MESH,
            )
            copies.append(copy)
            pl.when(there(dx, dy))(copy.start)
        return copies

    def wait_halo(v):
        for k, (dx, dy) in enumerate(DIRS):
            @pl.when(there(-dx, -dy))
            def _(k=k, dx=dx, dy=dy):
                halos[v][k].wait_recv()
                if dx and dy:
                    for offset, width, row, columns in corner_strips(-dx, -dy, True, XO, YE):
                        vol[0][v, row, columns] = edge_in[v, k - 4, offset : offset + width]

    loads[0].wait()
    halos = [send_halo(0)]
    loads[1].wait()
    loads[2].wait()

    def make_target(row):
        vol[0][1, XO + row, YE : YE + cols] = lab[row].astype(jnp.float32) * conf[row]

    loop(0, rows, make_target, 8)
    halos.append(send_halo(1))

    def clear_grad(row):
        for i in range(STAGES + 1):
            base[i][row] = jnp.zeros((cols + 24, planes), jnp.float32)
            if 0 < i < STAGES:
                grad[i][row] = jnp.zeros((cols + 24, planes), jnp.float32)

    loop(XO - DEPTH - 1, XO + rows + DEPTH + 1, clear_grad)
    for i in range(STAGES):
        reach = STAGES - i
        for row in (XO - reach - 2, XO - reach - 1, XO + rows + reach, XO + rows + reach + 1):
            for kind in range(7):
                wgt[i, kind, row] = jnp.zeros((cols + 24, planes), jnp.float32)
        for row in (XO - 2, XO - 1, XO + rows, XO + rows + 1):
            hy[i, row] = jnp.zeros((span, planes), jnp.float32)
            for kind in range(3):
                wx[i, kind, row] = jnp.zeros((span, planes), jnp.float32)

    tile = jnp.zeros((8, planes), jnp.float32)

    def clear_sides(row):
        for i in range(STAGES):
            for kind in range(7):
                if i == 0 or kind == YU:
                    wgt[i, kind, row, 0:8] = tile
                if i == 0 or kind == YL:
                    wgt[i, kind, row, cols + 16 : cols + 24] = tile

    loop(XO - STAGES, XO + rows + STAGES, clear_sides)

    def clear_pools(row):
        for i in range(STAGES):
            hz[i, row, YW - 8 : YW] = tile
            hz[i, row, YW + cols : YW + cols + 8] = tile
            for kind in range(3):
                wy[i, kind, row, YW - 8 : YW] = tile
                wy[i, kind, row, YW + cols : YW + cols + 8] = tile

    loop(0, rows, clear_pools)

    def stand_in(i, v):
        reach = DEPTH - i
        every = pl.ds(XO - reach, rows + 2 * reach)

        @pl.when(gy == 0)
        def _():
            vol[i][v, every, YE - 1 : YE] = vol[i][v, every, YE : YE + 1]

        @pl.when(gy == ngy - 1)
        def _():
            vol[i][v, every, YE + cols : YE + cols + 1] = vol[i][v, every, YE + cols - 1 : YE + cols]

        @pl.when(gx == 0)
        def _():
            vol[i][v, XO - 1] = vol[i][v, XO]

        @pl.when(gx == ngx - 1)
        def _():
            vol[i][v, XO + rows] = vol[i][v, XO + rows - 1]

    def before(value, edge):
        return jnp.where(at_first, edge, pltpu.roll(value, 1, 1))

    def after(value):
        return jnp.where(at_last, value, pltpu.roll(value, planes - 1, 1))

    def erode_step(i, v):
        reach = STAGES - i
        done = vol[i + 1]
        held = {}

        def at(row):
            if row not in held:
                held[row] = vol[i][v, row, 4 : 4 + span]
            return held[row]

        def eroded(row):
            mid = at(row)
            least = jnp.minimum(at(row - 1), at(row + 1))
            sides = jnp.minimum(vol[i][v, row, 3 : 3 + span], vol[i][v, row, 5 : 5 + span])
            along = jnp.minimum(before(mid, mid), after(mid))
            return jnp.minimum(jnp.minimum(least, sides), jnp.minimum(along, mid))

        def step(row):
            value = eroded(row)
            if row == XO - 1:
                value = jnp.where(gx == 0, eroded(XO), value)
            if row == XO + rows:
                value = jnp.where(gx == ngx - 1, eroded(XO + rows - 1), value)
            done[v, row, 4 : 4 + span] = value
            for place, inner, found in ((YE - 1, YE, gy == 0), (YE + cols, YE + cols - 1, gy == ngy - 1)):
                done[v, row, place : place + 1] = jnp.where(
                    found, done[v, row, inner : inner + 1], done[v, row, place : place + 1]
                )

        return XO - reach, XO + rows + reach, step

    def delta_step(i, v):
        held = {}

        def across(row):
            if row not in held:
                low, mid, high = [vol[i + 1][v, row, YE + y : YE + y + cols] for y in (-1, 0, 1)]
                held[row] = jnp.maximum(jnp.maximum(low, mid), high)
            return held[row]

        def step(row):
            row_at = XO + row
            most = jnp.maximum(jnp.maximum(across(row_at - 1), across(row_at)), across(row_at + 1))
            most = jnp.maximum(jnp.maximum(before(most, most), most), after(most))
            delta = jnp.maximum(vol[i][v, XO + row, YE : YE + cols] - most, 0.0)
            if i == 0:
                result = delta
            else:
                old = skel[i - 1][v, row]
                result = old + jnp.maximum(delta - old * delta, 0.0)
            skel[i][v, row] = result
            if v == 0:
                dels[i, row] = delta

        return 0, rows, step

    def forward(v):
        wait_halo(v)
        stand_in(0, v)
        straight(erode_step(0, v))
        for i in range(1, STAGES):
            straight(erode_step(i, v), delta_step(i - 1, v))
        straight(delta_step(STAGES - 1, v))

    forward(0)
    forward(1)

    def add_up(row, sums):
        sum_a, sum_b, sum_c, sum_d = sums
        skel_pred, skel_target = skel[ITERS][0, row], skel[ITERS][1, row]
        return (
            sum_a + skel_pred * vol[0][1, XO + row, YE : YE + cols],
            sum_b + skel_pred,
            sum_c + skel_target * vol[0][0, XO + row, YE : YE + cols],
            sum_d + skel_target,
        )

    sums = (jnp.zeros((cols, planes), jnp.float32),) * 4
    for row in range(rows):
        sums = add_up(row, sums)
    part[...] = jnp.zeros_like(part)
    for k in range(4):
        part[k : k + 1] = jnp.sum(sums[k], axis=0, keepdims=True)

    slots_y[gy] = part[...]
    copies_y = []
    for k in range(1, ngy):
        copy = pltpu.make_async_remote_copy(
            src_ref=part, dst_ref=slots_y.at[gy], send_sem=sy_send.at[k], recv_sem=sy_recv.at[k],
            device_id=(gx, lax.rem(gy + k, ngy)), device_id_type=MESH,
        )
        copy.start()
        copies_y.append(copy)

    def split(total, low, mid, high, first, sign):
        to_high = share(high, first) if sign > 0 else share(first, high)
        to_low = share(low, mid) if sign > 0 else share(mid, low)
        high_part = total * to_high
        rest = total - high_part
        low_part = rest * to_low
        return low_part, high_part, rest - low_part

    def dilate_weights(row):
        for i in range(STAGES):
            low, mid, high = [vol[i + 1][0, XO + row + x, 4 : 4 + span] for x in (-1, 0, 1)]
            first = jnp.maximum(low, mid)
            to_low, to_high, to_mid = split(1.0, low, mid, high, first, -1)
            wx[i, LO, XO + row] = to_low
            wx[i, UP, XO + row] = to_high
            wx[i, MID, XO + row] = to_mid
            pool[i, row] = jnp.maximum(first, high)

    loop(0, rows, dilate_weights, 4)

    def dilate_weights_2(row):
        below = 1.0
        for i in reversed(range(STAGES)):
            low, mid, high = [pool[i, row, 4 + y : 4 + y + cols] for y in (-1, 0, 1)]
            first = jnp.maximum(low, mid)
            to_low, to_high, to_mid = split(1.0, low, mid, high, first, -1)
            wy[i, LO, row, YW : YW + cols] = to_low
            wy[i, UP, row, YW : YW + cols] = to_high
            wy[i, MID, row, YW : YW + cols] = to_mid
            mid = jnp.maximum(first, high)
            low, high = before(mid, -jnp.inf), after(mid)
            first = jnp.maximum(low, mid)
            to_low, to_high, to_mid = split(1.0, low, mid, high, first, -1)
            wz[i, LO, row] = to_low
            wz[i, UP, row] = jnp.where(at_last, 0.0, to_high)
            wz[i, MID, row] = jnp.where(at_last, to_high + to_mid, to_mid)
            delta = dels[i, row]
            if i > 0:
                old = skel[i - 1][0, row]
                passed = jnp.where(delta - old * delta > 0.0, below, 0.0)
                coefs[i, row] = passed - passed * old
                below = below - passed * delta
            else:
                coefs[i, row] = jnp.where(delta > 0.0, below, 0.0)

    loop(0, rows, dilate_weights_2, 4)

    def erode_weights(i):
        reach = STAGES - i
        mine = slice(8, 8 + span)

        def step(row):
            mid = vol[i][0, row, 4 : 4 + span]
            x_low, x_high = vol[i][0, row - 1, 4 : 4 + span], vol[i][0, row + 1, 4 : 4 + span]
            y_low, y_high = vol[i][0, row, 3 : 3 + span], vol[i][0, row, 5 : 5 + span]
            z_low, z_high = before(mid, jnp.inf), after(mid)
            x_first, y_first, z_first = [jnp.minimum(low, mid) for low in (x_low, y_low, z_low)]
            x_pool, y_pool = jnp.minimum(x_first, x_high), jnp.minimum(y_first, y_high)
            z_pool = jnp.minimum(z_first, z_high)
            to_z = share(z_pool, jnp.minimum(x_pool, y_pool))
            rest = 1.0 - to_z
            to_y = rest * share(y_pool, x_pool)
            x_parts = split(rest - to_y, x_low, mid, x_high, x_first, 1)
            y_parts = split(to_y, y_low, mid, y_high, y_first, 1)
            z_parts = split(to_z, z_low, mid, z_high, z_first, 1)
            wgt[i, XL, row, mine] = x_parts[0]
            wgt[i, XU, row, mine] = x_parts[1]
            wgt[i, YL, row, mine] = y_parts[0]
            wgt[i, YU, row, mine] = y_parts[1]
            wgt[i, ZL, row, mine] = z_parts[0]
            wgt[i, ZU, row, mine] = jnp.where(at_last, 0.0, z_parts[1])
            centre = x_parts[2] + y_parts[2] + z_parts[2]
            wgt[i, CC, row, mine] = jnp.where(at_last, centre + z_parts[1], centre)

        halves((XO - reach, XO + rows + reach, step))

    def fold():
        mine = slice(8, 8 + span)

        def columns(edge, kind, pool_kind):
            at = pl.ds(edge, 1)
            for i in range(STAGES):
                reach = STAGES - i
                every = pl.ds(XO - reach, rows + 2 * reach)
                wgt[i, CC, every, at] = wgt[i, CC, every, at] + wgt[i, kind, every, at]
                wgt[i, kind, every, at] = jnp.zeros((rows + 2 * reach, 1, planes), jnp.float32)
                wy[i, MID, :, at] = wy[i, MID, :, at] + wy[i, pool_kind, :, at]
                wy[i, pool_kind, :, at] = jnp.zeros((rows, 1, planes), jnp.float32)

        def along_rows(edge, kind, pool_kind):
            for i in range(STAGES):
                wgt[i, CC, edge, mine] = wgt[i, CC, edge, mine] + wgt[i, kind, edge, mine]
                wgt[i, kind, edge, mine] = jnp.zeros((span, planes), jnp.float32)
                wx[i, MID, edge] = wx[i, MID, edge] + wx[i, pool_kind, edge]
                wx[i, pool_kind, edge] = jnp.zeros((span, planes), jnp.float32)

        pl.when(gy == 0)(lambda: columns(YW, YL, LO))
        pl.when(gy == ngy - 1)(lambda: columns(YW + cols - 1, YU, UP))
        pl.when(gx == 0)(lambda: along_rows(XO, XL, LO))
        pl.when(gx == ngx - 1)(lambda: along_rows(XO + rows - 1, XU, UP))

    erode_weights(0)

    for copy in copies_y:
        copy.wait()
    total = slots_y[0]
    for k in range(1, ngy):
        total = total + slots_y[k]
    part[...] = total
    slots_x[gx] = total
    copies_x = []
    for k in range(1, ngx):
        copy = pltpu.make_async_remote_copy(
            src_ref=part, dst_ref=slots_x.at[gx], send_sem=sx_send.at[k], recv_sem=sx_recv.at[k],
            device_id=(lax.rem(gx + k, ngx), gy), device_id_type=MESH,
        )
        copy.start()
        copies_x.append(copy)

    for i in range(1, STAGES):
        erode_weights(i)
    fold()

    for copy in copies_x:
        copy.wait()
    total = slots_x[0]
    for k in range(1, ngx):
        total = total + slots_x[k]
    sum_a, sum_b, sum_c, sum_d = [jnp.sum(total[k : k + 1], axis=1, keepdims=True) for k in range(4)]
    precision = (sum_a + 1.0) / (sum_b + 1.0)
    sensitivity = (sum_c + 1.0) / (sum_d + 1.0)
    together = precision + sensitivity
    loss[...] = 1.0 - 2.0 * precision * sensitivity / together
    cells = float(rows * ngx * cols * ngy * planes)
    coef_pred = cells * (-2.0 * sensitivity * sensitivity / (together * together)) / (sum_b + 1.0)
    coef_target = cells * (-2.0 * precision * precision / (together * together)) / (sum_d + 1.0)
    precision, coef_pred, coef_target = [
        jnp.broadcast_to(value, (cols, planes)) for value in (precision, coef_pred, coef_target)
    ]

    def start_back(row):
        cotangent = coef_pred * (vol[0][1, XO + row, YE : YE + cols] - precision)
        for i in range(STAGES):
            given = cotangent * coefs[i, row]
            base[i][XO + row, YW : YW + cols] = given
            hz[i, row, YW : YW + cols] = -(
                given * wz[i, MID, row]
                + pltpu.roll(given * wz[i, LO, row], planes - 1, 1)
                + pltpu.roll(given * wz[i, UP, row], 1, 1)
            )

    straight((0, rows, start_back))

    def back_columns(row):
        for i in range(STAGES):
            hy[i, XO + row] = (
                wy[i, MID, row, 8 : 8 + span] * hz[i, row, 8 : 8 + span]
                + wy[i, LO, row, 9 : 9 + span] * hz[i, row, 9 : 9 + span]
                + wy[i, UP, row, 7 : 7 + span] * hz[i, row, 7 : 7 + span]
            )

    straight((0, rows, back_columns))

    def back_rows(row):
        for i in range(STAGES):
            base[i + 1][row, 8 : 8 + span] = base[i + 1][row, 8 : 8 + span] + (
                wx[i, MID, row] * hy[i, row]
                + wx[i, LO, row + 1] * hy[i, row + 1]
                + wx[i, UP, row - 1] * hy[i, row - 1]
            )

    straight((XO - 1, XO + rows + 1, back_rows))

    def gather(i, row, low, length, held):
        source = grad[i + 1] if i + 1 < STAGES else base[i + 1]
        here = slice(low, low + length)
        up, down = slice(low + 1, low + 1 + length), slice(low - 1, low - 1 + length)

        def at(row):
            if row not in held:
                held[row] = source[row, here]
            return held[row]

        value = at(row)
        return (
            base[i][row, here]
            + wgt[i, CC, row, here] * value
            + wgt[i, XL, row + 1, here] * at(row + 1)
            + wgt[i, XU, row - 1, here] * at(row - 1)
            + wgt[i, YL, row, up] * source[row, up]
            + wgt[i, YU, row, down] * source[row, down]
            + pltpu.roll(wgt[i, ZL, row, here] * value, planes - 1, 1)
            + pltpu.roll(wgt[i, ZU, row, here] * value, 1, 1)
        )

    for i in reversed(range(1, STAGES)):
        held = {}

        def step(row, i=i, held=held):
            grad[i][row, 8 : 8 + span] = gather(i, row, 8, span, held)

        straight((XO - DEPTH + i, XO + rows + DEPTH - i, step))

    held_sides = {}

    def last_step(row):
        final[row] = gather(0, row, YW - 8, cols + 16, held_sides)

    def send_back(k):
        dx, dy = DIRS[k]
        if dx and dy:
            for offset, width, row, columns in corner_strips(dx, dy, True, XO, YE):
                back_out[k - 4, offset : offset + width] = final[row, columns]
            source, place = back_out.at[k - 4], got_c.at[k - 4]
        else:
            source = final.at[strip(dx, rows, XO, DEPTH, True), strip(dy, cols, YE, 8, True)]
            place = got_x.at[k] if dx else got_y.at[k - 2]
        copy = pltpu.make_async_remote_copy(
            src_ref=source,
            dst_ref=place,
            send_sem=g_send.at[k],
            recv_sem=g_recv.at[k],
            device_id=(gx + dx, gy + dy),
            device_id_type=MESH,
        )
        pl.when(there(dx, dy))(copy.start)
        return copy

    returns = {}
    for side, low in enumerate((XO - DEPTH, XO + rows)):
        for row in range(low, low + DEPTH):
            last_step(row)
        returns[side] = send_back(side)
    for k in range(4, 8):
        returns[k] = send_back(k)

    held_low, held_high, held_own = {}, {}, {}

    def side_columns(row):
        final[row, 0:YE] = gather(0, row, YW - YE, YE, held_low)
        final[row, YE + cols : cols + 16] = gather(0, row, YW + cols, 8, held_high)

    def middle_step(row):
        out[row] = gather(0, XO + row, YW, cols, held_own) + coef_target * skel[ITERS][1, row]

    straight((XO, XO + rows, side_columns))
    for k in (2, 3):
        returns[k] = send_back(k)
    straight((0, rows, middle_step))

    for k, (dx, dy) in enumerate(DIRS):
        @pl.when(there(-dx, -dy))
        def _(k=k, dx=dx, dy=dy):
            returns[k].wait_recv()
            if dx and dy:
                for offset, width, row, columns in corner_strips(-dx, -dy, False, 0, 0):
                    out[row, columns] = out[row, columns] + got_c[k - 4, offset : offset + width]
            else:
                at = (strip(-dx, rows, 0, DEPTH, False), strip(-dy, cols, 0, 8, False))
                out[at] = out[at] + (got_x[k] if dx else got_y[k - 2])

    for k, (dx, dy) in enumerate(DIRS):
        @pl.when(there(dx, dy))
        def _(k=k):
            halos[0][k].wait_send()
            halos[1][k].wait_send()
            returns[k].wait_send()


def body(prediction, label_mask, confidence):
    rows, cols, planes = prediction.shape
    ngx, ngy = lax.axis_size("gx"), lax.axis_size("gy")
    f32 = jnp.float32
    wide = rows + 2 * XO
    corner = (DEPTH * (DEPTH + 1) // 2 + 7) // 8 * 8
    dma = pltpu.SemaphoreType.DMA
    gradient, loss = pl.pallas_call(
        functools.partial(kernel, (rows, cols, planes, ngx, ngy)),
        out_shape=(jax.ShapeDtypeStruct((rows, cols, planes), f32), jax.ShapeDtypeStruct((1, 1), f32)),
        in_specs=[pl.BlockSpec(memory_space=pltpu.HBM)] * 3,
        out_specs=(pl.BlockSpec(memory_space=pltpu.VMEM), pl.BlockSpec(memory_space=pltpu.VMEM)),
        scratch_shapes=[
            [pltpu.VMEM((2, wide, cols + 16, planes), f32)] * (STAGES + 1),
            pltpu.VMEM((rows, cols, planes), jnp.int32),
            pltpu.VMEM((rows, cols, planes), f32),
            [pltpu.VMEM((2, rows, cols, planes), f32)] * STAGES,
            pltpu.VMEM((STAGES, rows, cols, planes), f32),
            pltpu.VMEM((STAGES, rows, cols, planes), f32),
            pltpu.VMEM((STAGES, rows, cols + 8, planes), f32),
            pltpu.VMEM((STAGES, 7, wide, cols + 24, planes), f32),
            pltpu.VMEM((STAGES, 3, wide, cols + 8, planes), f32),
            pltpu.VMEM((STAGES, 3, rows, cols + 24, planes), f32),
            pltpu.VMEM((STAGES, 3, rows, cols, planes), f32),
            [pltpu.VMEM((wide, cols + 24, planes), f32)] * (STAGES + 1),
            [pltpu.VMEM((wide, cols + 24, planes), f32)] * STAGES,
            pltpu.VMEM((STAGES, rows, cols + 24, planes), f32),
            pltpu.VMEM((STAGES, wide, cols + 8, planes), f32),
            pltpu.VMEM((wide, cols + 16, planes), f32),
            pltpu.VMEM((8, planes), f32),
            pltpu.VMEM((ngy, 8, planes), f32),
            pltpu.VMEM((ngx, 8, planes), f32),
            pltpu.VMEM((2, DEPTH, cols, planes), f32),
            pltpu.VMEM((2, rows, 8, planes), f32),
            pltpu.VMEM((4, corner, planes), f32),
            pltpu.VMEM((2, 4, corner, planes), f32),
            pltpu.VMEM((2, 4, corner, planes), f32),
            pltpu.VMEM((4, corner, planes), f32),
            dma((3,)),
            dma((16,)),
            dma((16,)),
            dma((ngy,)),
            dma((ngy,)),
            dma((ngx,)),
            dma((ngx,)),
            dma((8,)),
            dma((8,)),
        ],
        compiler_params=pltpu.CompilerParams(
            collective_id=0, has_side_effects=True, vmem_limit_bytes=50 * 1024 * 1024
        ),
    )(*(pltpu.with_memory_space_constraint(value, pltpu.HBM) for value in (prediction, label_mask, confidence)))
    return gradient, loss[0, 0]


def solution(mesh):
    placed = (P("gx", "gy", None), P("gx", "gy", None), P("gx", "gy", None))
    return jax.shard_map(
        body, mesh=mesh, in_specs=placed, out_specs=(P("gx", "gy", None), P()), check_vma=False
    )
```
